32 devices in a mesh: grp: 2 (over x), exp: 16 (over z, y, core).
Axes of the slice: x: 2, y: 2, z: 4, core: 2. Of those that a mesh axis runs over, the one named last changes fastest.
Arguments:
- tokens: bfloat16 [4096, 2048], P(('grp', 'exp')), parts along dimension 0, may hold values from -6 to 6
- expert_ids: int32 [4096, 8], P(('grp', 'exp')), parts along dimension 0, may hold values from 0 to 63, all different within a row; in each aligned block of 128 rows (0 to 127, 128 to 255, ...) at most 24 rows name the same one
- route_weight: float32 [4096, 8], P(('grp', 'exp')), parts along dimension 0, may hold values from 0.05 to 0.5
- w_gate: bfloat16 [64, 2048, 768], P('exp'), may hold values from -0.125 to 0.125
- w_up: bfloat16 [64, 2048, 768], P('exp'), may hold values from -0.125 to 0.125
- w_down: bfloat16 [64, 768, 2048], P('exp'), may hold values from -0.21875 to 0.21875
Outputs:
- mixed: bfloat16 [4096, 2048], P(('grp', 'exp')), parts along dimension 0
The draws below stay inside these ranges and needn't reach their ends.
There are 2 independent parts, one for each index of `grp`. The reference program is written for one: setup_inputs(seed, part) draws one part's arguments, and reference() takes and returns one part's arrays. A program takes and returns all parts, laid end to end along the dimension named above; an argument that names none is the same for every part. Nothing has to cross between parts.
Inputs may be any that keep to these rules, and one draw needn't show every extreme that they name: `expert_ids`: among the rows of one device (aligned blocks of 128 tokens) no expert is named more than 24 times, a bound that some block reaches; the experts of one token differ.
All inputs are finite; a program needn't handle non-finite values.
Results may differ from the reference program's by a relative error of at most 0.0057.
Values may be sent and summed in bfloat16 or wider, within the bound.
No kernel may reach another device: no remote copies, remote signals or barrier semaphores. Data moves between devices by JAX's collectives and lax.ppermute only.
A program may use at most 128 MiB of HBM per device.

```python
import math
import jax
import jax.numpy as jnp
import numpy as np
from jax import lax

D = 2048
FF = 768
EXPERTS = 64
TOPK = 8
TOK_DEV = 128
CAP = 24
TOKENS = 2048
N_EXP = 16


def block_levels(rng, dims, split, least, largest):
    def one(dim, parts):
        draws = jax.random.uniform(jax.random.fold_in(jax.random.fold_in(rng, 6), dim), (parts,), jnp.float32, least / len(split), largest / len(split))
        return jnp.repeat(jnp.exp(draws), dims[dim] // parts).reshape((-1,) + (1,) * (len(dims) - dim - 1))

    loudness = one(*split[0])
    for cut in split[1:]:
        loudness = loudness * one(*cut)
    return loudness


def shared_out(stream_key, own, number, rows, amount, top, limit, skew):
    order = jax.random.permutation(stream_key, amount)
    packed, usual = shares(amount, rows * top, limit, skew, True), shares(amount, rows * top, limit, skew, False)
    places = jnp.arange(amount)

    def named(lengths, rotation):
        used = int((lengths > 0).sum())
        fixed = max(1, used // 4)
        shifted = fixed + (places - fixed + rotation * (used - fixed)) % max(1, amount - fixed)
        return jnp.zeros((amount,), jnp.int32).at[order[jnp.where(places < fixed, places, shifted)]].set(jnp.asarray(lengths, jnp.int32))

    lengths = jnp.where(number % 4 == 0, named(packed, number // 4), named(usual, number - number // 4 - 1))
    mixed = jax.random.permutation(jax.random.fold_in(own, 3), amount)
    giver, taker = mixed[0:amount // 2 * 2:2], mixed[1:amount // 2 * 2:2]
    slack = jnp.minimum(lengths[giver] - 1, limit - lengths[taker]) // 2
    slack = jnp.where((giver == order[0]) | (taker == order[0]) | (lengths[taker] == 0), 0, jnp.maximum(slack, 0))
    shifted = jax.random.randint(jax.random.fold_in(own, 4), (amount // 2,), 0, 1 << 20) % (slack + 1)
    lengths = lengths.at[giver].add(-shifted).at[taker].add(shifted)
    labels = jnp.searchsorted(jnp.cumsum(lengths), jnp.arange(rows * top), side="right").astype(jnp.int32)
    grid = labels.reshape(top, rows).T
    grid = grid[jax.random.permutation(jax.random.fold_in(own, 1), rows)]
    rotation = jax.random.randint(jax.random.fold_in(own, 2), (rows, 1), 0, top)
    return jnp.take_along_axis(grid, (jnp.arange(top)[None, :] + rotation) % top, axis=1)


def shares(number_of, total, reach, lean, full):
    portions = [(1 << 20) // math.isqrt(standing ** lean) + 1 for standing in range(1, number_of + 1)]
    largest = reach if full else min(reach, max(-(-total // number_of), total * portions[0] // sum(portions)))
    least = 1 if total - largest >= number_of - 1 else 0
    given, rest = [largest] + [least] * (number_of - 1), total - largest - least * (number_of - 1)
    while rest > 0:
        movable = [i for i in range(1, number_of) if given[i] < largest] or [i for i in range(1, number_of) if given[i] < reach]
        whole, budget = sum([portions[i] for i in movable]), rest
        for i in movable:
            addition = min(reach - given[i], max(1, budget * portions[i] // whole), rest)
            given[i] = given[i] + addition
            rest = rest - addition
    return np.array(given)


def bell_draw(key, extent, scale, limit, pieces=(), kind=jnp.bfloat16):
    loudness = block_levels(key, extent, pieces, -0.22, 0.18) if pieces else 1.0
    values = jax.random.normal(key, extent, jnp.float32) * scale * loudness
    return jnp.minimum(jnp.maximum(values, -limit), limit).astype(kind)


def setup_inputs(seed: int = 0, part: int = 0) -> dict:
    key_of = jax.random.split(jax.random.key(seed), 7)
    own_keys = jax.random.split(jax.random.fold_in(key_of[6], part), 7)
    tokens = bell_draw(own_keys[0], (TOKENS, D), 1.0, 6.0, ((0, 16),))
    expert_ids_keys = jax.random.split(jax.random.fold_in(own_keys[1], 1), TOKENS // TOK_DEV)
    expert_ids_turns = jax.random.permutation(jax.random.fold_in(own_keys[1], 3), TOKENS // TOK_DEV)
    expert_ids = jax.vmap(lambda own, number: shared_out(jax.random.fold_in(own_keys[1], 2), own, number, TOK_DEV, EXPERTS, TOPK, CAP, 2))(expert_ids_keys, expert_ids_turns).reshape((TOKENS, TOPK))
    route_weight = jnp.clip(jnp.exp(math.log(0.5) - 2.3025851 * jax.random.uniform(own_keys[2], (TOKENS, TOPK), jnp.float32) ** block_levels(own_keys[2], (TOKENS, TOPK), ((0, 16),), -0.2, 0.2)), 0.05, 0.5)
    w_gate = bell_draw(key_of[3], (EXPERTS, D, FF), D ** -0.5, 0.125, ((0, 16),))
    w_up = bell_draw(key_of[4], (EXPERTS, D, FF), D ** -0.5, 0.125, ((0, 16),))
    w_down = bell_draw(key_of[5], (EXPERTS, FF, D), FF ** -0.5, 0.21875, ((0, 16),))
    return dict(tokens=tokens, expert_ids=expert_ids, route_weight=route_weight, w_gate=w_gate, w_up=w_up, w_down=w_down)


def expert_apply(operands):
    rows, gate_w, up_w, down_w = operands
    gate = jnp.dot(rows, gate_w, preferred_element_type=jnp.float32)
    up = jnp.dot(rows, up_w, preferred_element_type=jnp.float32)
    hidden = (jax.nn.silu(gate) * up).astype(jnp.bfloat16)
    return jnp.dot(hidden, down_w, preferred_element_type=jnp.float32).astype(jnp.bfloat16)


def reference(tokens, expert_ids, route_weight, w_gate, w_up, w_down):
    per_block = TOK_DEV * TOPK
    block_ids = expert_ids.reshape(N_EXP, per_block).astype(jnp.int32)
    onehot = (block_ids[:, :, None] == jnp.arange(EXPERTS, dtype=jnp.int32)[None, None, :]).astype(jnp.int32)
    before = jnp.cumsum(onehot, axis=1) - onehot
    slot_of = jnp.sum(before * onehot, axis=2)
    block_start = (jnp.arange(N_EXP, dtype=jnp.int32) * CAP)[:, None]
    dest_pos = (block_ids * (N_EXP * CAP) + block_start + slot_of).reshape(TOKENS * TOPK)
    token_of = jnp.arange(TOKENS * TOPK, dtype=jnp.int32) // TOPK
    row_index = jnp.full((EXPERTS * N_EXP * CAP,), TOKENS, jnp.int32).at[dest_pos].set(token_of)
    padded = jnp.concatenate([tokens, jnp.zeros((1, D), tokens.dtype)], axis=0)
    buffers = padded[row_index].reshape(EXPERTS, N_EXP * CAP, D)
    outputs = lax.map(expert_apply, (buffers, w_gate, w_up, w_down))
    results = outputs.reshape(EXPERTS * N_EXP * CAP, D)[dest_pos].reshape(TOKENS, TOPK, D)
    mixed = jnp.sum(results.astype(jnp.float32) * route_weight[:, :, None], axis=1)
    return mixed.astype(jnp.bfloat16)
```

```python
import functools

import jax
import jax.numpy as jnp
from jax import lax
from jax.experimental import pallas as pl
from jax.experimental.pallas import tpu as pltpu
from jax.sharding import PartitionSpec as P

CAP = 24
CORES = 2
VMEM_LIMIT = 48 * 1024 * 1024


def params(**kw):
    return pltpu.CompilerParams(vmem_limit_bytes=VMEM_LIMIT, **kw)


def selector(code_ref, local):
    row = jnp.concatenate([code_ref[0, local : local + 1, :], code_ref[1, local : local + 1, :] + CAP], axis=1)
    slots = lax.broadcasted_iota(jnp.int32, (2 * CAP, row.shape[1]), 0)
    return row == slots


def dispatch_kernel(code_ref, wt_ref, x0_ref, x1_ref, rows_ref, weight_ref):
    local_experts = rows_ref.shape[0]
    picks = []
    for local in range(local_experts):
        hit = selector(code_ref, local)
        wt = jnp.concatenate([wt_ref[0, local : local + 1, :], wt_ref[1, local : local + 1, :]], axis=1)
        weight = jnp.sum(jnp.where(hit, wt, 0.0), axis=1, keepdims=True)
        weight_ref[local] = jnp.broadcast_to(weight, weight_ref.shape[1:])
        picks.append(jnp.where(hit, 1.0, 0.0).astype(jnp.bfloat16))
    pick = jnp.concatenate(picks, axis=0)
    x = jnp.concatenate([x0_ref[...], x1_ref[...]], axis=0)
    rows = jnp.dot(pick, x, preferred_element_type=jnp.float32).astype(jnp.bfloat16)
    rows_ref[...] = rows.reshape(rows_ref.shape)


def dispatch(code, wt, x0, x1):
    local_experts = code.shape[1]
    width = x0.shape[1]
    return pl.pallas_call(
        dispatch_kernel,
        out_shape=(
            jax.ShapeDtypeStruct((local_experts, 2 * CAP, width), jnp.bfloat16),
            jax.ShapeDtypeStruct((local_experts, 2 * CAP, 128), jnp.float32),
        ),
        compiler_params=params(),
        cost_estimate=pl.CostEstimate(
            flops=2 * local_experts * 2 * CAP * 2 * x0.shape[0] * width,
            bytes_accessed=2 * width * (2 * x0.shape[0] + local_experts * 2 * CAP),
            transcendentals=0,
        ),
    )(code, wt, x0, x1)


def ffn_kernel(pairs, *refs):
    rows_refs, weight_refs = refs[:pairs], refs[pairs : 2 * pairs]
    gate_w, up_w, down_w, out_ref, total = refs[2 * pairs :]
    step = pl.program_id(1)
    rows = jnp.concatenate([r[0] for r in rows_refs], axis=0)
    weight = jnp.concatenate([r[0, :, :1] for r in weight_refs], axis=0)
    gate = jnp.dot(rows, gate_w[0], preferred_element_type=jnp.float32)
    up = jnp.dot(rows, up_w[0], preferred_element_type=jnp.float32)
    hidden = (gate / (1.0 + jnp.exp(-gate)) * up * weight).astype(jnp.bfloat16)
    part = jnp.dot(hidden, down_w[0], preferred_element_type=jnp.float32)

    @pl.when(step == 0)
    def _():
        total[...] = part

    @pl.when(step > 0)
    def _():
        total[...] += part

    @pl.when(step == pl.num_programs(1) - 1)
    def _():
        out_ref[...] = total[...].astype(jnp.bfloat16).reshape(out_ref.shape)


def ffn(rows, weights, w_gate, w_up, w_down):
    pairs = len(rows)
    local_experts, width, hidden = w_gate.shape
    block = 256 if hidden % 256 == 0 else hidden
    count = pairs * 2 * CAP
    return pl.pallas_call(
        functools.partial(ffn_kernel, pairs),
        grid=(local_experts, hidden // block),
        in_specs=[pl.BlockSpec((1, 2 * CAP, width), lambda l, f: (l, 0, 0))] * pairs
        + [pl.BlockSpec((1, 2 * CAP, 128), lambda l, f: (l, 0, 0))] * pairs
        + [
            pl.BlockSpec((1, width, block), lambda l, f: (l, 0, f)),
            pl.BlockSpec((1, width, block), lambda l, f: (l, 0, f)),
            pl.BlockSpec((1, block, width), lambda l, f: (l, f, 0)),
        ],
        out_specs=pl.BlockSpec((pairs, 1, 2 * CAP, width), lambda l, f: (0, l, 0, 0)),
        out_shape=jax.ShapeDtypeStruct((pairs, local_experts, 2 * CAP, width), jnp.bfloat16),
        scratch_shapes=[pltpu.VMEM((count, width), jnp.float32)],
        compiler_params=params(),
        cost_estimate=pl.CostEstimate(
            flops=6 * local_experts * count * width * hidden,
            bytes_accessed=6 * local_experts * width * hidden + 4 * local_experts * count * width,
            transcendentals=local_experts * count * hidden,
        ),
    )(*rows, *weights, w_gate, w_up, w_down)


def combine_kernel(code_ref, out_ref, y0_ref, y1_ref):
    local_experts = out_ref.shape[1]
    pick = jnp.concatenate(
        [jnp.where(selector(code_ref, l), 1.0, 0.0).astype(jnp.bfloat16) for l in range(local_experts)], axis=0
    )
    out = out_ref[0].reshape(local_experts * 2 * CAP, out_ref.shape[3])
    y = lax.dot_general(pick, out, (((0,), (0,)), ((), ())), preferred_element_type=jnp.float32)
    y = y.astype(jnp.bfloat16)
    y0_ref[...] = y[: y0_ref.shape[0]]
    y1_ref[...] = y[y0_ref.shape[0] :]


def combine(code, results, pair):
    _, local_experts, slots, width = results.shape
    tok = code.shape[2]
    shape = jax.ShapeDtypeStruct((tok, width), jnp.bfloat16)
    return pl.pallas_call(
        combine_kernel,
        grid=(1,),
        in_specs=[
            pl.BlockSpec(code.shape, lambda i: (0, 0, 0)),
            pl.BlockSpec((1, local_experts, slots, width), lambda i: (pair, 0, 0, 0)),
        ],
        out_specs=(pl.BlockSpec((tok, width), lambda i: (0, 0)),) * 2,
        out_shape=(shape, shape),
        compiler_params=params(),
        cost_estimate=pl.CostEstimate(
            flops=4 * local_experts * slots * tok * width,
            bytes_accessed=2 * width * (2 * tok + local_experts * slots),
            transcendentals=0,
        ),
    )(code, results)


def body(depth, lines, tokens, expert_ids, route_weight, w_gate, w_up, w_down):
    tok, width = tokens.shape
    local_experts = w_gate.shape[0]
    index = lax.axis_index("exp")
    z, y, core = index // (lines * CORES), index // CORES % lines, index % CORES

    def place(pz, py, pc):
        return (pz * lines + py) * CORES + pc

    everyone = [(a, b, c) for a in range(depth) for b in range(lines) for c in range(CORES)]

    def send(value, move, who=lambda a: True):
        perm = [(place(a, b, c), place(*move(a, b, c))) for a, b, c in everyone if who(a)]
        return lax.ppermute(value, "exp", perm)

    def swap_core(value):
        return send(value, lambda a, b, c: (a, b, 1 - c))

    def swap_line(value, who=lambda a: True):
        return send(value, lambda a, b, c: (a, 1 - b, c), who)

    def step_up(value, distance):
        return send(value, lambda a, b, c: (a + 1, b, c), lambda a: distance - 1 <= a < depth - 1)

    def step_down(value, distance):
        return send(value, lambda a, b, c: (a - 1, b, c), lambda a: 0 < a <= depth - distance)

    table = jnp.concatenate([expert_ids.T.astype(jnp.float32), route_weight.T], axis=0)
    table = lax.all_gather(table, "exp", axis=0)
    order = [(r, b, c) for r in range(depth) for b in range(lines) for c in range(CORES)]
    source = jnp.stack([place((z + r) % depth, y ^ b, core ^ c) for r, b, c in order])
    table = jnp.take(table, source, axis=0)
    top = expert_ids.shape[1]
    mine = (index * local_experts + jnp.arange(local_experts, dtype=jnp.int32)).astype(jnp.float32)
    hit = table[:, None, :top, :] == mine[None, :, None, None]
    member = jnp.sum(hit.astype(jnp.float32), axis=2)
    wt = jnp.sum(jnp.where(hit, table[:, None, top:, :], 0.0), axis=2)
    before = jnp.triu(jnp.ones((tok, tok), jnp.bfloat16), 1)
    rank = jnp.einsum("nlt,tu->nlu", member.astype(jnp.bfloat16), before, preferred_element_type=jnp.float32)
    code = jnp.where(member > 0.0, rank.astype(jnp.int32), -1024)

    above, below = [tokens], [tokens]
    across_above, across_below = [None], [None]
    if lines > 1:
        across = swap_line(tokens)
    for d in range(1, depth):
        below.append(step_up(below[-1], d))
        above.append(step_down(above[-1], d))
        if lines > 1:
            across_below.append(swap_line(below[-1], lambda a, d=d: a >= d))
            across_above.append(swap_line(above[-1], lambda a, d=d: a + d < depth))
    pieces = []
    for r in range(depth):
        if r == 0:
            pieces.append(tokens)
        else:
            pieces.append(jnp.where(z + r < depth, above[r], below[depth - r]))
        if lines > 1:
            if r == 0:
                pieces.append(across)
            else:
                pieces.append(jnp.where(z + r < depth, across_above[r], across_below[depth - r]))
    rows, weights = [], []
    for p, piece in enumerate(pieces):
        a, w = dispatch(code[2 * p : 2 * p + 2], wt[2 * p : 2 * p + 2], piece, swap_core(piece))
        rows.append(a)
        weights.append(w)

    results = ffn(rows, weights, w_gate, w_up, w_down)

    wide = jnp.float32
    link = jnp.bfloat16 if depth <= 4 else wide
    sums = [None] * depth
    first = []
    for d in range(depth - 1, 0, -1):
        for r in (d, depth - d):
            if r not in first:
                first.append(r)
    for r in first + [0]:
        halves = []
        for b in reversed(range(lines)):
            p = r * lines + b
            y0, y1 = combine(code[2 * p : 2 * p + 2], results, p)
            halves.append(y0.astype(wide) + swap_core(y1).astype(wide))
        own = halves[-1]
        if lines > 1:
            own = own + swap_line(halves[0].astype(jnp.bfloat16)).astype(wide)
        sums[r] = own
    up, down = sums[depth - 1] if depth > 1 else None, sums[1] if depth > 1 else None
    mixed = sums[0]
    for d in range(depth - 1, 0, -1):
        got_up = send(up.astype(link), lambda a, b, c: (a + 1, b, c), lambda a, d=d: a + d < depth).astype(wide)
        got_down = send(down.astype(link), lambda a, b, c: (a - 1, b, c), lambda a, d=d: a - d >= 0).astype(wide)
        if d > 1:
            up, down = sums[d - 1] + got_up, sums[depth - d + 1] + got_down
        else:
            mixed = mixed + got_up + got_down
    return mixed.astype(jnp.bfloat16)


def solution(mesh):
    groups, owners = mesh.shape["grp"], mesh.shape["exp"]
    lines = max(1, 4 // groups)
    depth = owners // (lines * CORES)
    in_specs = (
        P(("grp", "exp"), None),
        P(("grp", "exp"), None),
        P(("grp", "exp"), None),
        P("exp", None, None),
        P("exp", None, None),
        P("exp", None, None),
    )
    out_specs = P(("grp", "exp"), None)
    return jax.shard_map(
        functools.partial(body, depth, lines),
        mesh=mesh,
        in_specs=in_specs,
        out_specs=out_specs,
        check_vma=False,
    )
```

```python
import functools

import jax
import jax.numpy as jnp
from jax import lax
from jax.experimental import pallas as pl
from jax.experimental.pallas import tpu as pltpu
from jax.sharding import PartitionSpec as P

CAP = 24
CORES = 2
CHUNKS = 2
VMEM_LIMIT = 40 * 1024 * 1024


def params(**kw):
    return pltpu.CompilerParams(vmem_limit_bytes=VMEM_LIMIT, **kw)


def selector(code_ref, local):
    row = jnp.concatenate([code_ref[0, local : local + 1, :], code_ref[1, local : local + 1, :] + CAP], axis=1)
    slots = lax.broadcasted_iota(jnp.int32, (2 * CAP, row.shape[1]), 0)
    return row == slots


def dispatch_kernel(code_ref, wt_ref, x0_ref, x1_ref, rows_ref, weight_ref):
    local_experts = rows_ref.shape[0]
    picks = []
    for local in range(local_experts):
        hit = selector(code_ref, local)
        wt = jnp.concatenate([wt_ref[0, local : local + 1, :], wt_ref[1, local : local + 1, :]], axis=1)
        weight = jnp.sum(jnp.where(hit, wt, 0.0), axis=1, keepdims=True)
        weight_ref[local] = jnp.broadcast_to(weight, weight_ref.shape[1:])
        picks.append(jnp.where(hit, 1.0, 0.0).astype(jnp.bfloat16))
    pick = jnp.concatenate(picks, axis=0)
    x = jnp.concatenate([x0_ref[...], x1_ref[...]], axis=0)
    rows = jnp.dot(pick, x, preferred_element_type=jnp.float32).astype(jnp.bfloat16)
    rows_ref[...] = rows.reshape(rows_ref.shape)


def dispatch(code, wt, x0, x1):
    local_experts = code.shape[1]
    width = x0.shape[1]
    return pl.pallas_call(
        dispatch_kernel,
        out_shape=(
            jax.ShapeDtypeStruct((local_experts, 2 * CAP, width), jnp.bfloat16),
            jax.ShapeDtypeStruct((local_experts, 2 * CAP, 128), jnp.float32),
        ),
        compiler_params=params(),
        cost_estimate=pl.CostEstimate(
            flops=2 * local_experts * 2 * CAP * 2 * x0.shape[0] * width,
            bytes_accessed=2 * width * (2 * x0.shape[0] + local_experts * 2 * CAP),
            transcendentals=0,
        ),
    )(code, wt, x0, x1)


def rows_specs(rows):
    return [pl.BlockSpec((1,) + r.shape[1:], lambda l: (l, 0, 0)) for r in rows]


def joined(refs):
    return jnp.concatenate([r[0] for r in refs], axis=0)


def begin_kernel(pairs, *refs):
    rows = joined(refs[:pairs])
    gate_w, up_w, gate_ref, up_ref = refs[pairs:]
    gate_ref[0] = jnp.dot(rows, gate_w[0], preferred_element_type=jnp.float32)
    up_ref[0] = jnp.dot(rows, up_w[0], preferred_element_type=jnp.float32)


def begin(rows, w_gate, w_up):
    pairs = len(rows)
    local_experts, _, hidden = w_gate.shape
    count, width = pairs * rows[0].shape[1], rows[0].shape[2]
    weight_spec = pl.BlockSpec((1, width, hidden), lambda l: (l, 0, 0))
    sum_spec = pl.BlockSpec((1, count, hidden), lambda l: (l, 0, 0))
    shape = jax.ShapeDtypeStruct((local_experts, count, hidden), jnp.float32)
    return pl.pallas_call(
        functools.partial(begin_kernel, pairs),
        grid=(local_experts,),
        in_specs=rows_specs(rows) + [weight_spec] * 2,
        out_specs=(sum_spec, sum_spec),
        out_shape=(shape, shape),
        compiler_params=params(),
        cost_estimate=pl.CostEstimate(
            flops=4 * local_experts * count * width * hidden,
            bytes_accessed=4 * local_experts * width * hidden + 8 * local_experts * count * hidden,
            transcendentals=0,
        ),
    )(*rows, w_gate, w_up)


def middle_kernel(pairs, *refs):
    rows, weight = joined(refs[:pairs]), jnp.concatenate([r[0, :, :1] for r in refs[pairs : 2 * pairs]], axis=0)
    gate_sum, up_sum, gate_w, up_w, down_w, hidden_ref = refs[2 * pairs : 2 * pairs + 6]
    out_refs = refs[2 * pairs + 6 :]
    gate = gate_sum[0] + jnp.dot(rows, gate_w[0], preferred_element_type=jnp.float32)
    up = up_sum[0] + jnp.dot(rows, up_w[0], preferred_element_type=jnp.float32)
    hidden = (gate / (1.0 + jnp.exp(-gate)) * up * weight).astype(jnp.bfloat16)
    hidden_ref[0] = hidden
    write_out(out_refs, jnp.dot(hidden, down_w[0], preferred_element_type=jnp.float32))


def write_out(out_refs, out):
    out = out.astype(jnp.bfloat16)
    for p, ref in enumerate(out_refs):
        ref[0] = out[p * 2 * CAP : (p + 1) * 2 * CAP]


def middle(rows, weights, gate_sum, up_sum, w_gate, w_up, w_down):
    pairs = len(rows)
    local_experts, _, hidden = w_gate.shape
    count, width = pairs * rows[0].shape[1], rows[0].shape[2]
    weight_spec = pl.BlockSpec((1, width, hidden), lambda l: (l, 1, 0))
    sum_spec = pl.BlockSpec((1, count, hidden), lambda l: (l, 0, 0))
    out_shapes = [jax.ShapeDtypeStruct((local_experts, 2 * CAP, width), jnp.bfloat16)] * pairs
    got = pl.pallas_call(
        functools.partial(middle_kernel, pairs),
        grid=(local_experts,),
        in_specs=rows_specs(rows)
        + rows_specs(weights)
        + [sum_spec] * 2
        + [weight_spec] * 2
        + [pl.BlockSpec((1, hidden, width), lambda l: (l, 0, 0))],
        out_specs=[sum_spec] + rows_specs(out_shapes),
        out_shape=[jax.ShapeDtypeStruct((local_experts, count, hidden), jnp.bfloat16)] + out_shapes,
        compiler_params=params(),
        cost_estimate=pl.CostEstimate(
            flops=6 * local_experts * count * width * hidden,
            bytes_accessed=6 * local_experts * width * hidden + 8 * local_experts * count * hidden,
            transcendentals=local_experts * count * hidden,
        ),
    )(*rows, *weights, gate_sum, up_sum, w_gate, w_up, w_down)
    return got[0], got[1:]


def finish_kernel(hidden_ref, down_w, *out_refs):
    write_out(out_refs, jnp.dot(hidden_ref[0], down_w[0], preferred_element_type=jnp.float32))


def finish(hidden, w_down, width, pairs):
    local_experts, count, depth = hidden.shape
    out_shapes = [jax.ShapeDtypeStruct((local_experts, 2 * CAP, width), jnp.bfloat16)] * pairs
    return pl.pallas_call(
        finish_kernel,
        grid=(local_experts,),
        in_specs=[
            pl.BlockSpec((1, count, depth), lambda l: (l, 0, 0)),
            pl.BlockSpec((1, depth, width), lambda l: (l, 0, 1)),
        ],
        out_specs=rows_specs(out_shapes),
        out_shape=out_shapes,
        compiler_params=params(),
        cost_estimate=pl.CostEstimate(
            flops=2 * local_experts * count * width * depth,
            bytes_accessed=2 * local_experts * (width * depth + count * depth + count * width),
            transcendentals=0,
        ),
    )(hidden, w_down)


def combine_kernel(code_ref, out_ref, y0_ref, y1_ref):
    local_experts, slots, width = out_ref.shape
    pick = jnp.concatenate(
        [jnp.where(selector(code_ref, l), 1.0, 0.0).astype(jnp.bfloat16) for l in range(local_experts)], axis=0
    )
    out = out_ref[...].reshape(local_experts * slots, width)
    y = lax.dot_general(pick, out, (((0,), (0,)), ((), ())), preferred_element_type=jnp.float32)
    y0_ref[...] = y[: y0_ref.shape[0]]
    y1_ref[...] = y[y0_ref.shape[0] :].astype(jnp.bfloat16)


def combine(code, results):
    local_experts, slots, width = results.shape
    tok = code.shape[2]
    return pl.pallas_call(
        combine_kernel,
        out_shape=(
            jax.ShapeDtypeStruct((tok, width), jnp.float32),
            jax.ShapeDtypeStruct((tok, width), jnp.bfloat16),
        ),
        compiler_params=params(),
        cost_estimate=pl.CostEstimate(
            flops=4 * local_experts * slots * tok * width,
            bytes_accessed=2 * width * (3 * tok + local_experts * slots),
            transcendentals=0,
        ),
    )(code, results)


def body(depth, lines, tokens, expert_ids, route_weight, w_gate, w_up, w_down):
    tok, width = tokens.shape
    local_experts = w_gate.shape[0]
    index = lax.axis_index("exp")
    owners = depth * lines * CORES
    part = width // CHUNKS

    def place(pz, py, pc):
        return (pz % depth * lines + py) * CORES + pc

    everyone = [(a, b, c) for a in range(depth) for b in range(lines) for c in range(CORES)]

    def send(value, move):
        return lax.ppermute(value, "exp", [(place(*who), place(*move(*who))) for who in everyone])

    def swap_core(value):
        return send(value, lambda a, b, c: (a, b, 1 - c))

    def swap_line(value):
        return send(value, lambda a, b, c: (a, 1 - b, c))

    def to_above(value):
        return send(value, lambda a, b, c: (a + 1, b, c))

    def to_below(value):
        return send(value, lambda a, b, c: (a - 1, b, c))

    table = jnp.concatenate([expert_ids.T.astype(jnp.float32), route_weight.T], axis=0)[None]
    bit = 1
    while bit < owners:
        table = jnp.concatenate(
            [table, lax.ppermute(table, "exp", [(i, i ^ bit) for i in range(owners)])], axis=0
        )
        bit *= 2
    z, y, core = index // (lines * CORES), index // CORES % lines, index % CORES
    source = jnp.stack([place(z + r, y ^ b, core ^ c) ^ index for r, b, c in everyone])
    table = jnp.take(table, source, axis=0)
    top = expert_ids.shape[1]
    mine = (index * local_experts + jnp.arange(local_experts, dtype=jnp.int32)).astype(jnp.float32)
    hit = table[:, None, :top, :] == mine[None, :, None, None]
    member = jnp.sum(hit.astype(jnp.float32), axis=2)
    wt = jnp.sum(jnp.where(hit, table[:, None, top:, :], 0.0), axis=2)
    before = jnp.triu(jnp.ones((tok, tok), jnp.bfloat16), 1)
    rank = jnp.einsum("nlt,tu->nlu", member.astype(jnp.bfloat16), before, preferred_element_type=jnp.float32)
    code = jnp.where(member > 0.0, rank.astype(jnp.int32), -1024)

    nearer = depth // 2
    line = [[tokens[:, c * part : (c + 1) * part] for c in range(CHUNKS)]] + [None] * (depth - 1)
    far = [None] * depth

    def chunked(move, values):
        return [move(v) for v in values]

    turns = []
    for d in range(1, nearer + 1):
        turns.append((d, d - 1, to_below))
        if depth - d > nearer:
            turns.append((depth - d, (depth - d + 1) % depth, to_above))
    if lines > 1:
        far[0] = chunked(swap_line, line[0])
    for r, before_r, move in turns:
        line[r] = chunked(move, line[before_r])
        if lines > 1:
            far[r] = chunked(swap_line, line[r])
    rows, weights = [[] for _ in range(CHUNKS)], []
    codes = [code[2 * p : 2 * p + 2] for p in range(owners // CORES)]
    wts = [wt[2 * p : 2 * p + 2] for p in range(owners // CORES)]
    for p in range(owners // CORES):
        piece = line[p // lines] if p % lines == 0 else far[p // lines]
        for c in range(CHUNKS):
            a, w = dispatch(codes[p], wts[p], piece[c], swap_core(piece[c]))
            rows[c].append(a)
            if c == 0:
                weights.append(w)

    gate_sum, up_sum = begin(rows[0], w_gate, w_up)
    hidden, out0 = middle(rows[1], weights, gate_sum, up_sum, w_gate, w_up, w_down)
    results = [out0, finish(hidden, w_down, part, len(weights))]

    wide = jnp.float32
    link = jnp.bfloat16 if depth <= 4 else wide
    mixed = []
    for c in range(CHUNKS):

        def across(r):
            halves = []
            for b in reversed(range(lines)):
                p = r * lines + b
                y0, y1 = combine(codes[p], results[c][p])
                halves.append(y0 + swap_core(y1).astype(wide))
            if lines > 1:
                return halves[1] + swap_line(halves[0].astype(jnp.bfloat16)).astype(wide)
            return halves[0]

        got_up = got_down = 0.0
        for d in range(nearer, 0, -1):
            got_up = to_above((across(d) + got_up).astype(link)).astype(wide)
            if depth - d > nearer:
                got_down = to_below((across(depth - d) + got_down).astype(link)).astype(wide)
        mixed.append((across(0) + got_up + got_down).astype(jnp.bfloat16))
    return jnp.concatenate(mixed, axis=1)


def solution(mesh):
    groups, owners = mesh.shape["grp"], mesh.shape["exp"]
    lines = max(1, 4 // groups)
    depth = owners // (lines * CORES)
    in_specs = (
        P(("grp", "exp"), None),
        P(("grp", "exp"), None),
        P(("grp", "exp"), None),
        P("exp", None, None),
        P("exp", None, None),
        P("exp", None, None),
    )
    out_specs = P(("grp", "exp"), None)
    return jax.shard_map(
        functools.partial(body, depth, lines),
        mesh=mesh,
        in_specs=in_specs,
        out_specs=out_specs,
        check_vma=False,
    )
```

```python
import functools

import jax
import jax.numpy as jnp
from jax import lax
from jax.experimental import pallas as pl
from jax.experimental.pallas import tpu as pltpu
from jax.sharding import PartitionSpec as P

CAP = 24
CORES = 2
LANES = 128
VMEM_LIMIT = 40 * 1024 * 1024


def params(**kw):
    return pltpu.CompilerParams(vmem_limit_bytes=VMEM_LIMIT, **kw)


def selector(code_ref, local):
    row = jnp.concatenate([code_ref[0, local : local + 1, :], code_ref[1, local : local + 1, :] + CAP], axis=1)
    slots = lax.broadcasted_iota(jnp.int32, (2 * CAP, row.shape[1]), 0)
    return row == slots


def picks(code_ref):
    hits = [selector(code_ref, local) for local in range(code_ref.shape[1])]
    return jnp.concatenate([jnp.where(hit, 1.0, 0.0).astype(jnp.bfloat16) for hit in hits], axis=0)


def with_routes(tokens, expert_ids, route_weight):
    high = route_weight.astype(jnp.bfloat16)
    rest = route_weight - high.astype(jnp.float32)
    middle = rest.astype(jnp.bfloat16)
    low = (rest - middle.astype(jnp.float32)).astype(jnp.bfloat16)
    routes = jnp.concatenate([expert_ids.astype(jnp.bfloat16), high, middle, low], axis=1)
    return jnp.concatenate([jnp.pad(routes, ((0, 0), (0, LANES - routes.shape[1]))), tokens], axis=1)


def dispatch_kernel(top, first_ref, x0_ref, x1_ref, rows_ref, code_ref, weight_ref):
    local_experts = rows_ref.shape[0]
    tok = x0_ref.shape[0]
    first = first_ref[0]
    members, wts = [], []
    for x_ref in (x0_ref, x1_ref):
        routes = x_ref[:, :LANES].astype(jnp.float32).T
        ids = routes[:top].astype(jnp.int32)
        wt = routes[top : 2 * top] + (routes[2 * top : 3 * top] + routes[3 * top : 4 * top])
        for local in range(local_experts):
            hit = ids == first + local
            members.append(jnp.sum(jnp.where(hit, 1.0, 0.0), axis=0, keepdims=True))
            wts.append(jnp.sum(jnp.where(hit, wt, 0.0), axis=0, keepdims=True))
    pad = -len(members) % 16
    member = jnp.concatenate(members + [jnp.zeros((pad, tok), jnp.float32)] * (pad > 0), axis=0)
    before = lax.broadcasted_iota(jnp.int32, (tok, tok), 0) < lax.broadcasted_iota(jnp.int32, (tok, tok), 1)
    rank = jnp.dot(
        member.astype(jnp.bfloat16),
        jnp.where(before, 1.0, 0.0).astype(jnp.bfloat16),
        preferred_element_type=jnp.float32,
    )
    code = jnp.where(member > 0.0, rank.astype(jnp.int32), -1024)
    for i in range(2):
        for local in range(local_experts):
            n = i * local_experts + local
            code_ref[i, local : local + 1, :] = code[n : n + 1]
    for local in range(local_experts):
        wt = jnp.concatenate([wts[local], wts[local_experts + local]], axis=1)
        weight = jnp.sum(jnp.where(selector(code_ref, local), wt, 0.0), axis=1, keepdims=True)
        weight_ref[local] = jnp.broadcast_to(weight, weight_ref.shape[1:])
    pick_rows(code_ref, x0_ref[:, LANES:], x1_ref[:, LANES:], rows_ref)


def pick_rows(code_ref, x0, x1, rows_ref):
    x = jnp.concatenate([x0, x1], axis=0)
    rows = jnp.dot(picks(code_ref), x, preferred_element_type=jnp.float32).astype(jnp.bfloat16)
    rows_ref[...] = rows.reshape(rows_ref.shape)


def more_kernel(code_ref, x0_ref, x1_ref, rows_ref):
    pick_rows(code_ref, x0_ref[...], x1_ref[...], rows_ref)


def pick_cost(local_experts, tok, width):
    return pl.CostEstimate(
        flops=8 * local_experts * CAP * tok * width,
        bytes_accessed=4 * width * (tok + local_experts * CAP),
        transcendentals=0,
    )


def dispatch(first, top, local_experts, x0, x1):
    tok, width = x0.shape[0], x0.shape[1] - LANES
    whole = pl.BlockSpec(memory_space=pltpu.VMEM)
    return pl.pallas_call(
        functools.partial(dispatch_kernel, top),
        in_specs=[pl.BlockSpec(memory_space=pltpu.SMEM), whole, whole],
        out_specs=(whole,) * 3,
        out_shape=(
            jax.ShapeDtypeStruct((local_experts, 2 * CAP, width), jnp.bfloat16),
            jax.ShapeDtypeStruct((2, local_experts, tok), jnp.int32),
            jax.ShapeDtypeStruct((local_experts, 2 * CAP, LANES), jnp.float32),
        ),
        compiler_params=params(),
        cost_estimate=pick_cost(local_experts, tok, width),
    )(first, x0, x1)


def dispatch_more(code, x0, x1):
    local_experts, width = code.shape[1], x0.shape[1]
    return pl.pallas_call(
        more_kernel,
        out_shape=jax.ShapeDtypeStruct((local_experts, 2 * CAP, width), jnp.bfloat16),
        compiler_params=params(),
        cost_estimate=pick_cost(local_experts, x0.shape[0], width),
    )(code, x0, x1)


def column_specs(rows, part, chunk):
    def spec(r):
        at = chunk if r.shape[2] > part else 0
        return pl.BlockSpec((1, r.shape[1], part), lambda l: (l, 0, at))

    return [spec(r) for r in rows]


def rows_specs(rows):
    return [pl.BlockSpec((1,) + r.shape[1:], lambda l: (l, 0, 0)) for r in rows]


def joined(refs):
    return jnp.concatenate([r[0] for r in refs], axis=0)


def begin_kernel(pairs, *refs):
    rows = joined(refs[:pairs])
    gate_w, up_w, gate_ref, up_ref = refs[pairs:]
    gate_ref[0] = jnp.dot(rows, gate_w[0], preferred_element_type=jnp.float32)
    up_ref[0] = jnp.dot(rows, up_w[0], preferred_element_type=jnp.float32)


def begin(rows, width, w_gate, w_up):
    pairs = len(rows)
    local_experts, _, hidden = w_gate.shape
    count = pairs * rows[0].shape[1]
    weight_spec = pl.BlockSpec((1, width, hidden), lambda l: (l, 0, 0))
    sum_spec = pl.BlockSpec((1, count, hidden), lambda l: (l, 0, 0))
    shape = jax.ShapeDtypeStruct((local_experts, count, hidden), jnp.float32)
    return pl.pallas_call(
        functools.partial(begin_kernel, pairs),
        grid=(local_experts,),
        in_specs=column_specs(rows, width, 0) + [weight_spec] * 2,
        out_specs=(sum_spec, sum_spec),
        out_shape=(shape, shape),
        compiler_params=params(),
        cost_estimate=pl.CostEstimate(
            flops=4 * local_experts * count * width * hidden,
            bytes_accessed=4 * local_experts * width * hidden + 8 * local_experts * count * hidden,
            transcendentals=0,
        ),
    )(*rows, w_gate, w_up)


def middle_kernel(pairs, *refs):
    rows, weight = joined(refs[:pairs]), jnp.concatenate([r[0, :, :1] for r in refs[pairs : 2 * pairs]], axis=0)
    gate_sum, up_sum, gate_w, up_w, down_w, hidden_ref = refs[2 * pairs : 2 * pairs + 6]
    out_refs = refs[2 * pairs + 6 :]
    gate = gate_sum[0] + jnp.dot(rows, gate_w[0], preferred_element_type=jnp.float32)
    up = up_sum[0] + jnp.dot(rows, up_w[0], preferred_element_type=jnp.float32)
    hidden = (gate / (1.0 + jnp.exp(-gate)) * up * weight).astype(jnp.bfloat16)
    hidden_ref[0] = hidden
    write_out(out_refs, jnp.dot(hidden, down_w[0], preferred_element_type=jnp.float32))


def write_out(out_refs, out):
    out = out.astype(jnp.bfloat16)
    for p, ref in enumerate(out_refs):
        ref[0] = out[p * 2 * CAP : (p + 1) * 2 * CAP]


def middle(rows, width, weights, gate_sum, up_sum, w_gate, w_up, w_down):
    pairs = len(rows)
    local_experts, _, hidden = w_gate.shape
    count = pairs * rows[0].shape[1]
    weight_spec = pl.BlockSpec((1, width, hidden), lambda l: (l, 1, 0))
    sum_spec = pl.BlockSpec((1, count, hidden), lambda l: (l, 0, 0))
    out_shapes = [jax.ShapeDtypeStruct((local_experts, 2 * CAP, width), jnp.bfloat16)] * pairs
    got = pl.pallas_call(
        functools.partial(middle_kernel, pairs),
        grid=(local_experts,),
        in_specs=column_specs(rows, width, 1)
        + rows_specs(weights)
        + [sum_spec] * 2
        + [weight_spec] * 2
        + [pl.BlockSpec((1, hidden, width), lambda l: (l, 0, 0))],
        out_specs=[sum_spec] + rows_specs(out_shapes),
        out_shape=[jax.ShapeDtypeStruct((local_experts, count, hidden), jnp.bfloat16)] + out_shapes,
        compiler_params=params(),
        cost_estimate=pl.CostEstimate(
            flops=6 * local_experts * count * width * hidden,
            bytes_accessed=6 * local_experts * width * hidden + 8 * local_experts * count * hidden,
            transcendentals=local_experts * count * hidden,
        ),
    )(*rows, *weights, gate_sum, up_sum, w_gate, w_up, w_down)
    return got[0], got[1:]


def finish_kernel(hidden_ref, down_w, *out_refs):
    write_out(out_refs, jnp.dot(hidden_ref[0], down_w[0], preferred_element_type=jnp.float32))


def finish(hidden, w_down, width, pairs):
    local_experts, count, depth = hidden.shape
    out_shapes = [jax.ShapeDtypeStruct((local_experts, 2 * CAP, width), jnp.bfloat16)] * pairs
    return pl.pallas_call(
        finish_kernel,
        grid=(local_experts,),
        in_specs=[
            pl.BlockSpec((1, count, depth), lambda l: (l, 0, 0)),
            pl.BlockSpec((1, depth, width), lambda l: (l, 0, 1)),
        ],
        out_specs=rows_specs(out_shapes),
        out_shape=out_shapes,
        compiler_params=params(),
        cost_estimate=pl.CostEstimate(
            flops=2 * local_experts * count * width * depth,
            bytes_accessed=2 * local_experts * (width * depth + count * depth + count * width),
            transcendentals=0,
        ),
    )(hidden, w_down)


def combine_kernel(code_ref, *refs):
    out_refs, (y0_ref, y1_ref) = refs[:-2], refs[-2:]
    pick = picks(code_ref)
    for i, out_ref in enumerate(out_refs):
        local_experts, slots, width = out_ref.shape
        out = out_ref[...].reshape(local_experts * slots, width)
        y = lax.dot_general(pick, out, (((0,), (0,)), ((), ())), preferred_element_type=jnp.float32)
        tok = y0_ref.shape[0]
        y0_ref[:, i * width : (i + 1) * width] = y[:tok]
        y1_ref[:, i * width : (i + 1) * width] = y[tok:].astype(jnp.bfloat16)


def combine(code, *results):
    local_experts, slots, _ = results[0].shape
    width = sum(r.shape[2] for r in results)
    tok = code.shape[2]
    return pl.pallas_call(
        combine_kernel,
        out_shape=(
            jax.ShapeDtypeStruct((tok, width), jnp.float32),
            jax.ShapeDtypeStruct((tok, width), jnp.bfloat16),
        ),
        compiler_params=params(),
        cost_estimate=pl.CostEstimate(
            flops=4 * local_experts * slots * tok * width,
            bytes_accessed=2 * width * (3 * tok + local_experts * slots),
            transcendentals=0,
        ),
    )(code, *results)


def body(depth, lines, tokens, expert_ids, route_weight, w_gate, w_up, w_down):
    width = tokens.shape[1]
    top = expert_ids.shape[1]
    local_experts = w_gate.shape[0]
    index = lax.axis_index("exp")
    part = width // 2

    def place(pz, py, pc):
        return (pz % depth * lines + py) * CORES + pc

    everyone = [(a, b, c) for a in range(depth) for b in range(lines) for c in range(CORES)]

    def send(value, move):
        return lax.ppermute(value, "exp", [(place(*who), place(*move(*who))) for who in everyone])

    def swap_core(value):
        return send(value, lambda a, b, c: (a, b, 1 - c))

    def swap_line(value):
        return send(value, lambda a, b, c: (a, 1 - b, c))

    def to_above(value):
        return send(value, lambda a, b, c: (a + 1, b, c))

    def to_below(value):
        return send(value, lambda a, b, c: (a - 1, b, c))

    nearer = depth // 2
    line = [with_routes(tokens, expert_ids, route_weight)] + [None] * (depth - 1)
    turns = []
    for d in range(1, nearer + 1):
        turns.append((d, d - 1, to_below))
        if depth - d > nearer:
            turns.append((depth - d, (depth - d + 1) % depth, to_above))
    for r, source, move in turns:
        line[r] = move(line[source])
    pieces = {(r, 0): line[r] for r in range(depth)}
    if lines > 1:
        for r in [0] + [t[0] for t in turns[:-1]]:
            pieces[r, 1] = swap_line(line[r])
        pieces[nearer, 1] = [swap_line(v) for v in (line[nearer][:, : LANES + part], line[nearer][:, LANES + part :])]

    first = (index * local_experts).astype(jnp.int32).reshape(1)
    rows, codes, weights = {}, {}, {}
    for key, piece in pieces.items():
        halves = piece if isinstance(piece, list) else [piece]
        a, codes[key], weights[key] = dispatch(first, top, local_experts, halves[0], swap_core(halves[0]))
        rows[key] = [a, a]
        if len(halves) > 1:
            rows[key][1] = dispatch_more(codes[key], halves[1], swap_core(halves[1]))
    keys = list(rows)

    gate_sum, up_sum = begin([rows[k][0] for k in keys], part, w_gate, w_up)
    hidden, out0 = middle(
        [rows[k][1] for k in keys], part, [weights[k] for k in keys], gate_sum, up_sum, w_gate, w_up, w_down
    )
    out1 = finish(hidden, w_down, part, len(keys))
    results = {k: (out0[i], out1[i]) for i, k in enumerate(keys)}

    wide = jnp.float32
    link = jnp.bfloat16 if depth <= 4 else wide

    def across(r, parts=(0, 1)):
        halves = []
        for b in reversed(range(lines)):
            y0, y1 = combine(codes[r, b], *[results[r, b][i] for i in parts])
            halves.append(y0 + swap_core(y1).astype(wide))
        if lines > 1:
            return halves[1] + swap_line(halves[0].astype(jnp.bfloat16)).astype(wide)
        return halves[0]

    got_up = got_down = 0.0
    for d in range(nearer, 0, -1):
        if d == nearer:
            got_up = [to_above(across(d, (i,)).astype(link)).astype(wide) for i in range(2)]
            got_up = jnp.concatenate(got_up, axis=1)
        else:
            got_up = to_above((across(d) + got_up).astype(link)).astype(wide)
        if depth - d > nearer:
            got_down = to_below((across(depth - d) + got_down).astype(link)).astype(wide)
    return (across(0) + got_up + got_down).astype(jnp.bfloat16)


def solution(mesh):
    groups, owners = mesh.shape["grp"], mesh.shape["exp"]
    lines = max(1, 4 // groups)
    depth = owners // (lines * CORES)
    in_specs = (
        P(("grp", "exp"), None),
        P(("grp", "exp"), None),
        P(("grp", "exp"), None),
        P("exp", None, None),
        P("exp", None, None),
        P("exp", None, None),
    )
    out_specs = P(("grp", "exp"), None)
    return jax.shard_map(
        functools.partial(body, depth, lines),
        mesh=mesh,
        in_specs=in_specs,
        out_specs=out_specs,
        check_vma=False,
    )
```

```python
import functools

import jax
import jax.numpy as jnp
from jax import lax
from jax.experimental import pallas as pl
from jax.experimental.pallas import tpu as pltpu
from jax.sharding import PartitionSpec as P

CAP = 24
CORES = 2
LANES = 128
MIB = 1024 * 1024
SMALL_LIMIT = 6 * MIB


def params(limit=SMALL_LIMIT):
    return pltpu.CompilerParams(vmem_limit_bytes=limit)


def selector(code_ref, local):
    row = jnp.concatenate([code_ref[0, local : local + 1, :], code_ref[1, local : local + 1, :] + CAP], axis=1)
    slots = lax.broadcasted_iota(jnp.int32, (2 * CAP, row.shape[1]), 0)
    return row == slots


def picks(code_ref):
    hits = [selector(code_ref, local) for local in range(code_ref.shape[1])]
    return jnp.concatenate([jnp.where(hit, 1.0, 0.0).astype(jnp.bfloat16) for hit in hits], axis=0)


def with_routes(tokens, expert_ids, route_weight):
    high = route_weight.astype(jnp.bfloat16)
    rest = route_weight - high.astype(jnp.float32)
    middle = rest.astype(jnp.bfloat16)
    low = (rest - middle.astype(jnp.float32)).astype(jnp.bfloat16)
    routes = jnp.concatenate([expert_ids.astype(jnp.bfloat16), high, middle, low], axis=1)
    return jnp.concatenate([jnp.pad(routes, ((0, 0), (0, LANES - routes.shape[1]))), tokens], axis=1)


def dispatch_kernel(top, first_ref, x0_ref, x1_ref, rows_ref, code_ref, weight_ref):
    local_experts = rows_ref.shape[0]
    tok = x0_ref.shape[0]
    first = first_ref[0]
    members, wts = [], []
    for x_ref in (x0_ref, x1_ref):
        routes = x_ref[:, :LANES].astype(jnp.float32).T
        ids = routes[:top].astype(jnp.int32)
        wt = routes[top : 2 * top] + (routes[2 * top : 3 * top] + routes[3 * top : 4 * top])
        for local in range(local_experts):
            hit = ids == first + local
            members.append(jnp.sum(jnp.where(hit, 1.0, 0.0), axis=0, keepdims=True))
            wts.append(jnp.sum(jnp.where(hit, wt, 0.0), axis=0, keepdims=True))
    pad = -len(members) % 16
    member = jnp.concatenate(members + [jnp.zeros((pad, tok), jnp.float32)] * (pad > 0), axis=0)
    before = lax.broadcasted_iota(jnp.int32, (tok, tok), 0) < lax.broadcasted_iota(jnp.int32, (tok, tok), 1)
    rank = jnp.dot(
        member.astype(jnp.bfloat16),
        jnp.where(before, 1.0, 0.0).astype(jnp.bfloat16),
        preferred_element_type=jnp.float32,
    )
    code = jnp.where(member > 0.0, rank.astype(jnp.int32), -1024)
    for i in range(2):
        for local in range(local_experts):
            n = i * local_experts + local
            code_ref[i, local : local + 1, :] = code[n : n + 1]
    for local in range(local_experts):
        wt = jnp.concatenate([wts[local], wts[local_experts + local]], axis=1)
        weight = jnp.sum(jnp.where(selector(code_ref, local), wt, 0.0), axis=1, keepdims=True)
        weight_ref[local] = jnp.broadcast_to(weight, weight_ref.shape[1:])
    pick_rows(code_ref, x0_ref[:, LANES:], x1_ref[:, LANES:], rows_ref)


def pick_rows(code_ref, x0, x1, rows_ref):
    x = jnp.concatenate([x0, x1], axis=0)
    rows = jnp.dot(picks(code_ref), x, preferred_element_type=jnp.float32).astype(jnp.bfloat16)
    rows_ref[...] = rows.reshape(rows_ref.shape)


def more_kernel(code_ref, x0_ref, x1_ref, rows_ref):
    pick_rows(code_ref, x0_ref[...], x1_ref[...], rows_ref)


def pick_cost(local_experts, tok, width):
    return pl.CostEstimate(
        flops=8 * local_experts * CAP * tok * width,
        bytes_accessed=4 * width * (tok + local_experts * CAP),
        transcendentals=0,
    )


def dispatch(first, top, local_experts, x0, x1):
    tok, width = x0.shape[0], x0.shape[1] - LANES
    whole = pl.BlockSpec(memory_space=pltpu.VMEM)
    return pl.pallas_call(
        functools.partial(dispatch_kernel, top),
        in_specs=[pl.BlockSpec(memory_space=pltpu.SMEM), whole, whole],
        out_specs=(whole,) * 3,
        out_shape=(
            jax.ShapeDtypeStruct((local_experts, 2 * CAP, width), jnp.bfloat16),
            jax.ShapeDtypeStruct((2, local_experts, tok), jnp.int32),
            jax.ShapeDtypeStruct((local_experts, 2 * CAP, LANES), jnp.float32),
        ),
        compiler_params=params(),
        cost_estimate=pl.CostEstimate(flops=0, bytes_accessed=0, transcendentals=0),
    )(first, x0, x1)


def dispatch_more(code, x0, x1):
    local_experts, width = code.shape[1], x0.shape[1]
    return pl.pallas_call(
        more_kernel,
        out_shape=jax.ShapeDtypeStruct((local_experts, 2 * CAP, width), jnp.bfloat16),
        compiler_params=params(),
        cost_estimate=pl.CostEstimate(flops=0, bytes_accessed=0, transcendentals=0),
    )(code, x0, x1)


def row_blocks(pairs):
    return [range(p, min(p + 8, pairs)) for p in range(0, pairs, 8)]


def columns_of(refs, part, chunk):
    return [slice(chunk * part, (chunk + 1) * part) if r.shape[2] > part else slice(None) for r in refs]


def rows_of(refs, local, part, chunk, block):
    where = columns_of(refs, part, chunk)
    return jnp.concatenate([refs[p][local, :, where[p]] for p in block], axis=0)


def span(block):
    return slice(block[0] * 2 * CAP, (block[-1] + 1) * 2 * CAP)


class Stream:
    def __init__(self, hbm, buffer, sems, rows, columns):
        self.hbm, self.buffer, self.sems, self.where = hbm, buffer, sems, (rows, columns)

    def copy(self, local):
        slot = local % 2
        return pltpu.make_async_copy(self.hbm.at[(local,) + self.where], self.buffer.at[slot], self.sems.at[slot])

    def start(self, local):
        self.copy(local).start()

    def get(self, local):
        self.copy(local).wait()
        return self.buffer[local % 2]


def over_experts(count, streams, work):
    for stream in streams:
        stream.start(0)

    @pl.loop(0, count)
    def _(local):
        @pl.when(local + 1 < count)
        def _():
            for stream in streams:
                stream.start(local + 1)

        work(local)


def stream_scratch(*shapes):
    buffers = [pltpu.VMEM((2,) + shape, jnp.bfloat16) for shape in shapes]
    return buffers + [pltpu.SemaphoreType.DMA((2,)) for _ in shapes]


def begin_kernel(pairs, part, *refs):
    rows_refs = refs[:pairs]
    gate_hbm, up_hbm, gate_ref, up_ref, gate_buf, up_buf, gate_sem, up_sem = refs[pairs:]
    head, full = slice(0, part), slice(None)
    gate_w = Stream(gate_hbm, gate_buf, gate_sem, head, full)
    up_w = Stream(up_hbm, up_buf, up_sem, head, full)

    def work(local):
        blocks = row_blocks(pairs)
        for stream, out_ref in ((gate_w, gate_ref), (up_w, up_ref)):
            weight = stream.get(local)
            for block in blocks:
                rows = rows_of(rows_refs, local, part, 0, block)
                out_ref[local, span(block)] = jnp.dot(rows, weight, preferred_element_type=jnp.float32)

    over_experts(gate_ref.shape[0], (gate_w, up_w), work)


VMEM_SPEC = pl.BlockSpec(memory_space=pltpu.VMEM)
HBM_SPEC = pl.BlockSpec(memory_space=pltpu.HBM)


def begin(rows, part, w_gate, w_up):
    pairs = len(rows)
    local_experts, _, hidden = w_gate.shape
    count = pairs * 2 * CAP
    shape = jax.ShapeDtypeStruct((local_experts, count, hidden), jnp.float32)
    return pl.pallas_call(
        functools.partial(begin_kernel, pairs, part),
        in_specs=[VMEM_SPEC] * pairs + [HBM_SPEC] * 2,
        out_specs=(VMEM_SPEC,) * 2,
        out_shape=(shape, shape),
        scratch_shapes=stream_scratch((part, hidden), (part, hidden)),
        compiler_params=params(32 * MIB),
        cost_estimate=pl.CostEstimate(flops=0, bytes_accessed=0, transcendentals=0),
    )(*rows, w_gate, w_up)


def middle_kernel(pairs, part, *refs):
    rows_refs, weight_refs = refs[:pairs], refs[pairs : 2 * pairs]
    gate_sum, up_sum, gate_hbm, up_hbm, down_hbm, hidden_ref = refs[2 * pairs : 2 * pairs + 6]
    out_refs, scratch = refs[2 * pairs + 6 : 3 * pairs + 6], refs[3 * pairs + 6 :]
    tail, full = slice(part, 2 * part), slice(None)
    gate_w = Stream(gate_hbm, scratch[0], scratch[3], tail, full)
    up_w = Stream(up_hbm, scratch[1], scratch[4], tail, full)
    down_w = Stream(down_hbm, scratch[2], scratch[5], full, slice(0, part))

    def work(local):
        gate_now, up_now, down_now = gate_w.get(local), up_w.get(local), None
        for block in row_blocks(pairs):
            rows = rows_of(rows_refs, local, part, 1, block)
            weight = jnp.concatenate([weight_refs[p][local, :, :1] for p in block], axis=0)
            at = span(block)
            gate = gate_sum[local, at] + jnp.dot(rows, gate_now, preferred_element_type=jnp.float32)
            up = up_sum[local, at] + jnp.dot(rows, up_now, preferred_element_type=jnp.float32)
            hidden = (gate / (1.0 + jnp.exp(-gate)) * up * weight).astype(jnp.bfloat16)
            hidden_ref[local, at] = hidden
            if down_now is None:
                down_now = down_w.get(local)
            write_out(out_refs, local, block, hidden, down_now)

    over_experts(hidden_ref.shape[0], (gate_w, up_w, down_w), work)


def write_out(out_refs, local, block, hidden, weight):
    out = jnp.dot(hidden, weight, preferred_element_type=jnp.float32).astype(jnp.bfloat16)
    for i, p in enumerate(block):
        out_refs[p][local] = out[i * 2 * CAP : (i + 1) * 2 * CAP]


def middle(rows, part, weights, gate_sum, up_sum, w_gate, w_up, w_down):
    pairs = len(rows)
    local_experts, _, hidden = w_gate.shape
    count = pairs * 2 * CAP
    out_shapes = [jax.ShapeDtypeStruct((local_experts, 2 * CAP, part), jnp.bfloat16)] * pairs
    got = pl.pallas_call(
        functools.partial(middle_kernel, pairs, part),
        in_specs=[VMEM_SPEC] * (2 * pairs + 2) + [HBM_SPEC] * 3,
        out_specs=[VMEM_SPEC] * (pairs + 1),
        out_shape=[jax.ShapeDtypeStruct((local_experts, count, hidden), jnp.bfloat16)] + out_shapes,
        scratch_shapes=stream_scratch((part, hidden), (part, hidden), (hidden, part)),
        compiler_params=params(32 * MIB),
        cost_estimate=pl.CostEstimate(flops=0, bytes_accessed=0, transcendentals=0),
    )(*rows, *weights, gate_sum, up_sum, w_gate, w_up, w_down)
    return got[0], got[1:]


def finish_kernel(pairs, part, hidden_ref, down_hbm, *refs):
    out_refs, (buffer, sem) = refs[:pairs], refs[pairs:]
    down_w = Stream(down_hbm, buffer, sem, slice(None), slice(part, 2 * part))

    def work(local):
        weight = down_w.get(local)
        for block in row_blocks(pairs):
            write_out(out_refs, local, block, hidden_ref[local, span(block)], weight)

    over_experts(hidden_ref.shape[0], (down_w,), work)


def finish(hidden, w_down, part, pairs):
    local_experts, count, depth = hidden.shape
    return pl.pallas_call(
        functools.partial(finish_kernel, pairs, part),
        in_specs=[VMEM_SPEC, HBM_SPEC],
        out_specs=[VMEM_SPEC] * pairs,
        out_shape=[jax.ShapeDtypeStruct((local_experts, 2 * CAP, part), jnp.bfloat16)] * pairs,
        scratch_shapes=stream_scratch((depth, part)),
        compiler_params=params(46 * MIB),
        cost_estimate=pl.CostEstimate(flops=0, bytes_accessed=0, transcendentals=0),
    )(hidden, w_down)


def combine_kernel(code_ref, *refs):
    out_refs, (y0_ref, y1_ref) = refs[:-2], refs[-2:]
    pick = picks(code_ref)
    for i, out_ref in enumerate(out_refs):
        local_experts, slots, width = out_ref.shape
        out = out_ref[...].reshape(local_experts * slots, width)
        y = lax.dot_general(pick, out, (((0,), (0,)), ((), ())), preferred_element_type=jnp.float32)
        tok = y0_ref.shape[0]
        y0_ref[:, i * width : (i + 1) * width] = y[:tok]
        y1_ref[:, i * width : (i + 1) * width] = y[tok:].astype(jnp.bfloat16)


def combine(code, *results):
    local_experts, slots, _ = results[0].shape
    width = sum(r.shape[2] for r in results)
    tok = code.shape[2]
    return pl.pallas_call(
        combine_kernel,
        out_shape=(
            jax.ShapeDtypeStruct((tok, width), jnp.float32),
            jax.ShapeDtypeStruct((tok, width), jnp.bfloat16),
        ),
        compiler_params=params(),
        cost_estimate=pl.CostEstimate(flops=0, bytes_accessed=0, transcendentals=0),
    )(code, *results)


def after(value, *others):
    return lax.optimization_barrier((value, *others))[0]


def body(depth, lines, tokens, expert_ids, route_weight, w_gate, w_up, w_down):
    width = tokens.shape[1]
    top = expert_ids.shape[1]
    local_experts = w_gate.shape[0]
    index = lax.axis_index("exp")
    part = width // 2

    def place(pz, py, pc):
        return (pz % depth * lines + py) * CORES + pc

    everyone = [(a, b, c) for a in range(depth) for b in range(lines) for c in range(CORES)]

    def send(value, move):
        return lax.ppermute(value, "exp", [(place(*who), place(*move(*who))) for who in everyone])

    def swap_core(value):
        return send(value, lambda a, b, c: (a, b, 1 - c))

    def swap_line(value):
        return send(value, lambda a, b, c: (a, 1 - b, c))

    def to_above(value):
        return send(value, lambda a, b, c: (a + 1, b, c))

    def to_below(value):
        return send(value, lambda a, b, c: (a - 1, b, c))

    nearer = depth // 2
    line = [with_routes(tokens, expert_ids, route_weight)] + [None] * (depth - 1)
    turns = []
    for d in range(1, nearer + 1):
        turns.append((d, d - 1, to_below))
        if depth - d > nearer:
            turns.append((depth - d, (depth - d + 1) % depth, to_above))
    first = (index * local_experts).astype(jnp.int32).reshape(1)
    rows, codes, weights, late = {}, {}, {}, {}

    def take(key, piece):
        halves = piece if isinstance(piece, list) else [piece]
        a, codes[key], weights[key] = dispatch(first, top, local_experts, halves[0], swap_core(halves[0]))
        rows[key] = [a, a]
        if len(halves) > 1:
            late[key] = halves[1]

    for r, source, move in turns:
        line[r] = move(line[source])
    if lines > 1:
        far = {0: swap_line(line[0])}
        for r, _, _ in turns[:-1]:
            far[r] = swap_line(line[r])
        for r in [0] + [t[0] for t in turns[:-1]]:
            take((r, 0), line[r])
        for r in [0] + [t[0] for t in turns[:-2]]:
            take((r, 1), far[r])
        last = after(line[nearer], *[rows[k][0] for k in rows])
        far[nearer] = [swap_line(v) for v in (last[:, : LANES + part], last[:, LANES + part :])]
        for r in far:
            if (r, 1) not in rows:
                take((r, 1), far[r])
        take((nearer, 0), line[nearer])
    else:
        for r in range(depth):
            take((r, 0), line[r])
    keys = sorted(rows)

    gate_sum, up_sum = begin([rows[k][0] for k in keys], part, w_gate, w_up)
    for key, half in late.items():
        half, gate_sum, up_sum = lax.optimization_barrier((half, gate_sum, up_sum))
        rows[key][1] = dispatch_more(codes[key], half, swap_core(half))
    hidden, out0 = middle(
        [rows[k][1] for k in keys], part, [weights[k] for k in keys], gate_sum, up_sum, w_gate, w_up, w_down
    )
    out1 = finish(hidden, w_down, part, len(keys))
    results = {k: (out0[i], out1[i]) for i, k in enumerate(keys)}

    wide = jnp.float32
    link = jnp.bfloat16 if depth <= 4 else wide

    def across(r, parts=(0, 1)):
        halves = []
        for b in reversed(range(lines)):
            y0, y1 = combine(codes[r, b], *[results[r, b][i] for i in parts])
            halves.append(y0 + swap_core(y1).astype(wide))
        if lines > 1:
            return halves[1] + swap_line(halves[0].astype(jnp.bfloat16)).astype(wide)
        return halves[0]

    got_up = got_down = 0.0
    for d in range(nearer, 0, -1):
        if d == nearer:
            got_up = [to_above(across(d, (i,)).astype(link)).astype(wide) for i in range(2)]
            got_up = jnp.concatenate(got_up, axis=1)
        else:
            got_up = to_above((across(d) + got_up).astype(link)).astype(wide)
        if depth - d > nearer:
            got_down = to_below((across(depth - d) + got_down).astype(link)).astype(wide)
    return (across(0) + got_up + got_down).astype(jnp.bfloat16)


def solution(mesh):
    groups, owners = mesh.shape["grp"], mesh.shape["exp"]
    lines = max(1, 4 // groups)
    depth = owners // (lines * CORES)
    in_specs = (
        P(("grp", "exp"), None),
        P(("grp", "exp"), None),
        P(("grp", "exp"), None),
        P("exp", None, None),
        P("exp", None, None),
        P("exp", None, None),
    )
    out_specs = P(("grp", "exp"), None)
    return jax.shard_map(
        functools.partial(body, depth, lines),
        mesh=mesh,
        in_specs=in_specs,
        out_specs=out_specs,
        check_vma=False,
    )
```

```python
import functools

import jax
import jax.numpy as jnp
from jax import lax
from jax.experimental import pallas as pl
from jax.experimental.pallas import tpu as pltpu
from jax.sharding import PartitionSpec as P

CAP = 24
CORES = 2
LANES = 128
LONG = 40_000_000_000
MIB = 1024 * 1024
SMALL_LIMIT = 6 * MIB


def params(limit=SMALL_LIMIT):
    return pltpu.CompilerParams(vmem_limit_bytes=limit)


def selector(code_ref, local):
    row = jnp.concatenate([code_ref[0, local : local + 1, :], code_ref[1, local : local + 1, :] + CAP], axis=1)
    slots = lax.broadcasted_iota(jnp.int32, (2 * CAP, row.shape[1]), 0)
    return row == slots


def picks(code_ref):
    hits = [selector(code_ref, local) for local in range(code_ref.shape[1])]
    return jnp.concatenate([jnp.where(hit, 1.0, 0.0).astype(jnp.bfloat16) for hit in hits], axis=0)


def routes_kernel(ids_ref, weight_ref, tokens_ref, out_ref):
    top, tok = ids_ref.shape
    high = weight_ref[...].astype(jnp.bfloat16).astype(jnp.float32)
    rest = weight_ref[...] - high
    middle = rest.astype(jnp.bfloat16).astype(jnp.float32)
    routes = jnp.concatenate([ids_ref[...].astype(jnp.float32), high, middle, rest - middle], axis=0)
    out_ref[:, :LANES] = jnp.zeros((out_ref.shape[0], LANES), jnp.bfloat16)
    out_ref[: 4 * top, :tok] = routes.astype(jnp.bfloat16)
    out_ref[:, LANES:] = tokens_ref[...]


def with_routes(tokens, expert_ids, route_weight):
    tok, width = tokens.shape
    return pl.pallas_call(
        routes_kernel,
        out_shape=jax.ShapeDtypeStruct((tok, LANES + width), jnp.bfloat16),
        compiler_params=params(58 * MIB),
        cost_estimate=pl.CostEstimate(flops=0, bytes_accessed=0, transcendentals=0),
    )(expert_ids.T, route_weight.T, tokens)


def dispatch_kernel(top, first_ref, x0_ref, x1_ref, rows_ref, code_ref, weight_ref):
    local_experts = rows_ref.shape[0]
    tok = x0_ref.shape[0]
    first = first_ref[0]
    members, wts = [], []
    for x_ref in (x0_ref, x1_ref):
        routes = x_ref[: 4 * top, :tok].astype(jnp.float32)
        ids = routes[:top].astype(jnp.int32)
        wt = routes[top : 2 * top] + (routes[2 * top : 3 * top] + routes[3 * top : 4 * top])
        for local in range(local_experts):
            hit = ids == first + local
            members.append(jnp.sum(jnp.where(hit, 1.0, 0.0), axis=0, keepdims=True))
            wts.append(jnp.sum(jnp.where(hit, wt, 0.0), axis=0, keepdims=True))
    pad = -len(members) % 16
    member = jnp.concatenate(members + [jnp.zeros((pad, tok), jnp.float32)] * (pad > 0), axis=0)
    before = lax.broadcasted_iota(jnp.int32, (tok, tok), 0) < lax.broadcasted_iota(jnp.int32, (tok, tok), 1)
    rank = jnp.dot(
        member.astype(jnp.bfloat16),
        jnp.where(before, 1.0, 0.0).astype(jnp.bfloat16),
        preferred_element_type=jnp.float32,
    )
    code = jnp.where(member > 0.0, rank.astype(jnp.int32), -1024)
    for i in range(2):
        for local in range(local_experts):
            n = i * local_experts + local
            code_ref[i, local : local + 1, :] = code[n : n + 1]
    for local in range(local_experts):
        wt = jnp.concatenate([wts[local], wts[local_experts + local]], axis=1)
        weight = jnp.sum(jnp.where(selector(code_ref, local), wt, 0.0), axis=1, keepdims=True)
        weight_ref[local] = jnp.broadcast_to(weight, weight_ref.shape[1:])
    pick_rows(code_ref, x0_ref[:, LANES:], x1_ref[:, LANES:], rows_ref)


def pick_rows(code_ref, x0, x1, rows_ref):
    x = jnp.concatenate([x0, x1], axis=0)
    rows = jnp.dot(picks(code_ref), x, preferred_element_type=jnp.float32).astype(jnp.bfloat16)
    rows_ref[...] = rows.reshape(rows_ref.shape)


def more_kernel(code_ref, x0_ref, x1_ref, rows_ref):
    pick_rows(code_ref, x0_ref[...], x1_ref[...], rows_ref)


def pick_cost(local_experts, tok, width):
    return pl.CostEstimate(
        flops=8 * local_experts * CAP * tok * width,
        bytes_accessed=4 * width * (tok + local_experts * CAP),
        transcendentals=0,
    )


def dispatch(first, top, local_experts, x0, x1):
    tok, width = x0.shape[0], x0.shape[1] - LANES
    whole = pl.BlockSpec(memory_space=pltpu.VMEM)
    return pl.pallas_call(
        functools.partial(dispatch_kernel, top),
        in_specs=[pl.BlockSpec(memory_space=pltpu.SMEM), whole, whole],
        out_specs=(whole,) * 3,
        out_shape=(
            jax.ShapeDtypeStruct((local_experts, 2 * CAP, width), jnp.bfloat16),
            jax.ShapeDtypeStruct((2, local_experts, tok), jnp.int32),
            jax.ShapeDtypeStruct((local_experts, 2 * CAP, LANES), jnp.float32),
        ),
        compiler_params=params(),
        cost_estimate=pl.CostEstimate(flops=0, bytes_accessed=0, transcendentals=0),
    )(first, x0, x1)


def dispatch_more(code, x0, x1):
    local_experts, width = code.shape[1], x0.shape[1]
    return pl.pallas_call(
        more_kernel,
        out_shape=jax.ShapeDtypeStruct((local_experts, 2 * CAP, width), jnp.bfloat16),
        compiler_params=params(),
        cost_estimate=pl.CostEstimate(flops=0, bytes_accessed=0, transcendentals=0),
    )(code, x0, x1)


def row_blocks(pairs):
    return [range(p, min(p + 8, pairs)) for p in range(0, pairs, 8)]


def columns_of(refs, part, chunk):
    return [slice(chunk * part, (chunk + 1) * part) if r.shape[2] > part else slice(None) for r in refs]


def rows_of(refs, local, part, chunk, block):
    where = columns_of(refs, part, chunk)
    return jnp.concatenate([refs[p][local, :, where[p]] for p in block], axis=0)


def span(block):
    return slice(block[0] * 2 * CAP, (block[-1] + 1) * 2 * CAP)


class Stream:
    def __init__(self, hbm, buffer, sems, rows, columns):
        self.hbm, self.buffer, self.sems, self.where = hbm, buffer, sems, (rows, columns)

    def copy(self, local):
        slot = local % 2
        return pltpu.make_async_copy(self.hbm.at[(local,) + self.where], self.buffer.at[slot], self.sems.at[slot])

    def start(self, local):
        self.copy(local).start()

    def get(self, local):
        self.copy(local).wait()
        return self.buffer[local % 2]


def over_experts(count, streams, work):
    for stream in streams:
        stream.start(0)

    @pl.loop(0, count)
    def _(local):
        @pl.when(local + 1 < count)
        def _():
            for stream in streams:
                stream.start(local + 1)

        work(local)


def stream_scratch(*shapes):
    buffers = [pltpu.VMEM((2,) + shape, jnp.bfloat16) for shape in shapes]
    return buffers + [pltpu.SemaphoreType.DMA((2,)) for _ in shapes]


def begin_kernel(pairs, part, token_ref, *refs):
    rows_refs = refs[:pairs]
    gate_hbm, up_hbm, gate_ref, up_ref, gate_buf, up_buf, gate_sem, up_sem = refs[pairs:]
    head, full = slice(0, part), slice(None)
    gate_w = Stream(gate_hbm, gate_buf, gate_sem, head, full)
    up_w = Stream(up_hbm, up_buf, up_sem, head, full)

    def work(local):
        blocks = row_blocks(pairs)
        for stream, out_ref in ((gate_w, gate_ref), (up_w, up_ref)):
            weight = stream.get(local)
            for block in blocks:
                rows = rows_of(rows_refs, local, part, 0, block)
                out_ref[local, span(block)] = jnp.dot(rows, weight, preferred_element_type=jnp.float32)

    over_experts(gate_ref.shape[0], (gate_w, up_w), work)


VMEM_SPEC = pl.BlockSpec(memory_space=pltpu.VMEM)
HBM_SPEC = pl.BlockSpec(memory_space=pltpu.HBM)


def begin(token, rows, part, w_gate, w_up):
    pairs = len(rows)
    local_experts, _, hidden = w_gate.shape
    count = pairs * 2 * CAP
    shape = jax.ShapeDtypeStruct((local_experts, count, hidden), jnp.float32)
    return pl.pallas_call(
        functools.partial(begin_kernel, pairs, part),
        in_specs=[VMEM_SPEC] * (pairs + 1) + [HBM_SPEC] * 2,
        out_specs=(VMEM_SPEC,) * 2,
        out_shape=(shape, shape),
        scratch_shapes=stream_scratch((part, hidden), (part, hidden)),
        compiler_params=params(32 * MIB),
        cost_estimate=pl.CostEstimate(flops=LONG, bytes_accessed=0, transcendentals=0),
    )(token, *rows, w_gate, w_up)


def middle_kernel(pairs, part, *refs):
    rows_refs, weight_refs = refs[:pairs], refs[pairs : 2 * pairs]
    gate_sum, up_sum, gate_hbm, up_hbm, down_hbm, hidden_ref = refs[2 * pairs : 2 * pairs + 6]
    out_refs, scratch = refs[2 * pairs + 6 : 3 * pairs + 6], refs[3 * pairs + 6 :]
    tail, full = slice(part, 2 * part), slice(None)
    gate_w = Stream(gate_hbm, scratch[0], scratch[3], tail, full)
    up_w = Stream(up_hbm, scratch[1], scratch[4], tail, full)
    down_w = Stream(down_hbm, scratch[2], scratch[5], full, slice(0, part))

    def work(local):
        gate_now, up_now, down_now = gate_w.get(local), up_w.get(local), None
        for block in row_blocks(pairs):
            rows = rows_of(rows_refs, local, part, 1, block)
            weight = jnp.concatenate([weight_refs[p][local, :, :1] for p in block], axis=0)
            at = span(block)
            gate = gate_sum[local, at] + jnp.dot(rows, gate_now, preferred_element_type=jnp.float32)
            up = up_sum[local, at] + jnp.dot(rows, up_now, preferred_element_type=jnp.float32)
            hidden = (gate / (1.0 + jnp.exp(-gate)) * up * weight).astype(jnp.bfloat16)
            hidden_ref[local, at] = hidden
            if down_now is None:
                down_now = down_w.get(local)
            write_out(out_refs, local, block, hidden, down_now)

    over_experts(hidden_ref.shape[0], (gate_w, up_w, down_w), work)


def write_out(out_refs, local, block, hidden, weight):
    out = jnp.dot(hidden, weight, preferred_element_type=jnp.float32).astype(jnp.bfloat16)
    for i, p in enumerate(block):
        out_refs[p][local] = out[i * 2 * CAP : (i + 1) * 2 * CAP]


def middle(rows, part, weights, gate_sum, up_sum, w_gate, w_up, w_down):
    pairs = len(rows)
    local_experts, _, hidden = w_gate.shape
    count = pairs * 2 * CAP
    out_shapes = [jax.ShapeDtypeStruct((local_experts, 2 * CAP, part), jnp.bfloat16)] * pairs
    got = pl.pallas_call(
        functools.partial(middle_kernel, pairs, part),
        in_specs=[VMEM_SPEC] * (2 * pairs + 2) + [HBM_SPEC] * 3,
        out_specs=[VMEM_SPEC] * (pairs + 1),
        out_shape=[jax.ShapeDtypeStruct((local_experts, count, hidden), jnp.bfloat16)] + out_shapes,
        scratch_shapes=stream_scratch((part, hidden), (part, hidden), (hidden, part)),
        compiler_params=params(32 * MIB),
        cost_estimate=pl.CostEstimate(flops=0, bytes_accessed=0, transcendentals=0),
    )(*rows, *weights, gate_sum, up_sum, w_gate, w_up, w_down)
    return got[0], got[1:]


def finish_kernel(pairs, part, hidden_ref, down_hbm, *refs):
    out_refs, (buffer, sem) = refs[:pairs], refs[pairs:]
    down_w = Stream(down_hbm, buffer, sem, slice(None), slice(part, 2 * part))

    def work(local):
        weight = down_w.get(local)
        for block in row_blocks(pairs):
            write_out(out_refs, local, block, hidden_ref[local, span(block)], weight)

    over_experts(hidden_ref.shape[0], (down_w,), work)


def finish(hidden, w_down, part, pairs):
    local_experts, count, depth = hidden.shape
    return pl.pallas_call(
        functools.partial(finish_kernel, pairs, part),
        in_specs=[VMEM_SPEC, HBM_SPEC],
        out_specs=[VMEM_SPEC] * pairs,
        out_shape=[jax.ShapeDtypeStruct((local_experts, 2 * CAP, part), jnp.bfloat16)] * pairs,
        scratch_shapes=stream_scratch((depth, part)),
        compiler_params=params(46 * MIB),
        cost_estimate=pl.CostEstimate(flops=0, bytes_accessed=0, transcendentals=0),
    )(hidden, w_down)


def combine_kernel(code_ref, *refs):
    out_refs, (y0_ref, y1_ref) = refs[:-2], refs[-2:]
    pick = picks(code_ref)
    for i, out_ref in enumerate(out_refs):
        local_experts, slots, width = out_ref.shape
        out = out_ref[...].reshape(local_experts * slots, width)
        y = lax.dot_general(pick, out, (((0,), (0,)), ((), ())), preferred_element_type=jnp.float32)
        tok = y0_ref.shape[0]
        y0_ref[:, i * width : (i + 1) * width] = y[:tok]
        y1_ref[:, i * width : (i + 1) * width] = y[tok:].astype(jnp.bfloat16)


def combine(code, *results):
    local_experts, slots, _ = results[0].shape
    width = sum(r.shape[2] for r in results)
    tok = code.shape[2]
    return pl.pallas_call(
        combine_kernel,
        out_shape=(
            jax.ShapeDtypeStruct((tok, width), jnp.float32),
            jax.ShapeDtypeStruct((tok, width), jnp.bfloat16),
        ),
        compiler_params=params(),
        cost_estimate=pl.CostEstimate(flops=0, bytes_accessed=0, transcendentals=0),
    )(code, *results)


def after(value, *others):
    return lax.optimization_barrier((value, *others))[0]


def fence_kernel(in_ref, out_ref):
    out_ref[...] = in_ref[...] + 1.0


def tie(*values):
    return lax.optimization_barrier(values)


def fence(token, *later):
    token = pl.pallas_call(
        fence_kernel,
        out_shape=jax.ShapeDtypeStruct(token.shape, token.dtype),
        compiler_params=params(),
        cost_estimate=pl.CostEstimate(flops=LONG, bytes_accessed=0, transcendentals=0),
    )(token)
    return tie(token, *later)


def last_kernel(token_ref, a_ref, *refs):
    refs, out_ref = refs[:-1], refs[-1]
    total = a_ref[...]
    for ref in refs:
        total += ref[...].astype(jnp.float32)
    out_ref[...] = total.astype(out_ref.dtype)


def last_sum(token, *terms):
    return pl.pallas_call(
        last_kernel,
        in_specs=[VMEM_SPEC] * (1 + len(terms)),
        out_shape=jax.ShapeDtypeStruct(terms[0].shape, jnp.bfloat16),
        compiler_params=params(),
        cost_estimate=pl.CostEstimate(flops=0, bytes_accessed=0, transcendentals=0),
    )(token, *terms)


def body(depth, lines, tokens, expert_ids, route_weight, w_gate, w_up, w_down):
    width = tokens.shape[1]
    top = expert_ids.shape[1]
    local_experts = w_gate.shape[0]
    index = lax.axis_index("exp")
    part = width // 2

    def place(pz, py, pc):
        return (pz % depth * lines + py) * CORES + pc

    everyone = [(a, b, c) for a in range(depth) for b in range(lines) for c in range(CORES)]

    def send(value, move):
        return lax.ppermute(value, "exp", [(place(*who), place(*move(*who))) for who in everyone])

    def swap_core(value):
        return send(value, lambda a, b, c: (a, b, 1 - c))

    def swap_line(value):
        return send(value, lambda a, b, c: (a, 1 - b, c))

    def to_above(value):
        return send(value, lambda a, b, c: (a + 1, b, c))

    def to_below(value):
        return send(value, lambda a, b, c: (a - 1, b, c))

    nearer = depth // 2
    line = [with_routes(tokens, expert_ids, route_weight)] + [None] * (depth - 1)
    turns = []
    for d in range(1, nearer + 1):
        turns.append((d, d - 1, to_below))
        if depth - d > nearer:
            turns.append((depth - d, (depth - d + 1) % depth, to_above))
    first = (index * local_experts).astype(jnp.int32).reshape(1)
    rows, codes, weights, late = {}, {}, {}, {}

    def take(key, piece, other):
        halves = piece if isinstance(piece, list) else [piece]
        rows[key], codes[key], weights[key] = dispatch(first, top, local_experts, halves[0], other)
        if len(halves) > 1:
            late[key] = halves[1]

    if lines > 1 and depth == 4:
        line[1], far = to_below(line[0]), {0: swap_line(line[0])}
        others = {(0, 0): swap_core(line[0])}
        token, line[0] = fence(jnp.zeros((8, LANES), jnp.float32), line[0])
        line[3] = to_above(line[0])
        token, line[1], others[0, 0] = fence(token, line[1], others[0, 0])
        far[1], others[1, 0] = swap_line(line[1]), swap_core(line[1])
        token, line[1] = fence(token, line[1])
        line[2] = to_below(line[1])
        take((0, 0), line[0], others[0, 0])
        token, line[1], rows[0, 0] = tie(token, line[1], rows[0, 0])
        token, line[3], far[0], others[1, 0] = fence(token, line[3], far[0], others[1, 0])
        far[3] = swap_line(line[3])
        others[3, 0], others[0, 1] = swap_core(line[3]), swap_core(far[0])
        take((1, 0), line[1], others[1, 0])
        token, line[3], far[0], rows[1, 0] = tie(token, line[3], far[0], rows[1, 0])
        others[1, 1] = swap_core(far[1])
        token, line[2], others[3, 0], others[0, 1], others[1, 1] = fence(
            token, line[2], others[3, 0], others[0, 1], others[1, 1]
        )
        head, tail = swap_line(line[2][:, : LANES + part]), swap_line(line[2][:, LANES + part :])
        others[2, 0] = swap_core(line[2])
        for key, piece in (((3, 0), line[3]), ((0, 1), far[0]), ((1, 1), far[1])):
            take(key, piece, others[key])
        token, rows[3, 0], rows[0, 1], rows[1, 1] = tie(token, rows[3, 0], rows[0, 1], rows[1, 1])
        token, far[3], head = fence(token, far[3], head)
        others[3, 1], others[2, 1] = swap_core(far[3]), swap_core(head)
        take((2, 0), line[2], others[2, 0])
        take((3, 1), far[3], others[3, 1])
        take((2, 1), [head, tail], others[2, 1])
    else:
        token = jnp.zeros((8, LANES), jnp.float32)
        for r, source, move in turns:
            line[r] = move(line[source])
        for r in range(depth):
            take((r, 0), line[r], swap_core(line[r]))
            if lines > 1:
                piece = swap_line(line[r])
                take((r, 1), piece, swap_core(piece))
    keys = sorted(rows)

    gate_sum, up_sum = begin(token, [rows[k] for k in keys], part, w_gate, w_up)
    for key, half in late.items():
        half, gate_sum, up_sum = lax.optimization_barrier((half, gate_sum, up_sum))
        rows[key] = dispatch_more(codes[key], half, swap_core(half))
    hidden, out0 = middle(
        [rows[k] for k in keys], part, [weights[k] for k in keys], gate_sum, up_sum, w_gate, w_up, w_down
    )
    out0 = dict(zip(keys, out0))

    wide = jnp.float32
    link = jnp.bfloat16 if depth <= 4 else wide

    def chip_sums(r, *parts):
        sums = []
        for b in reversed(range(lines)):
            y0, y1 = combine(codes[r, b], *[part[r, b] for part in parts])
            sums.append(y0 + swap_core(y1).astype(wide))
        return sums[::-1]

    def lined(sums):
        return sums[0] + swap_line(sums[1].astype(link)).astype(wide) if lines > 1 else sums[0]

    if lines > 1 and depth == 4:
        early = chip_sums(2, out0)
        token, first_half, hidden = tie(token, early[1].astype(link), hidden)
        cross2 = swap_line(first_half)
        token, hidden = fence(token, hidden)
        out1 = dict(zip(keys, finish(hidden, w_down, part, len(keys))))
        token, out1[2, 1] = tie(token, out1[2, 1])
        rest = [(1, 0), (1, 1), (0, 0), (0, 1)]
        half, third = chip_sums(2, out1), chip_sums(3, out0, out1)
        aside, cross3, *tied = tie(half[1].astype(link), third[1].astype(link), *[codes[k] for k in rest])
        codes.update(zip(rest, tied))
        aside, cross3, ahead = to_above(aside), swap_line(cross3), to_above(half[0].astype(link))
        token, cross2 = fence(token, cross2)
        behind = to_above((early[0] + cross2).astype(link))
        nearest, own = chip_sums(1, out0, out1), chip_sums(0, out0, out1)
        token, aside = fence(token, aside)
        cross1 = jnp.concatenate([nearest[1][:, :part], nearest[1][:, part:] + aside], axis=1).astype(link)
        cross1 = swap_line(cross1)
        token, last, cross3 = fence(token, own[1].astype(link), cross3)
        below = to_below((third[0] + cross3).astype(link))
        cross0 = swap_line(last)
        token, cross1, behind, ahead = fence(token, cross1, behind, ahead)
        above = to_above((nearest[0] + cross1 + jnp.concatenate([behind, ahead], axis=1)).astype(link))
        return last_sum(token, own[0], cross0, above, below)

    out1 = dict(zip(keys, finish(hidden, w_down, part, len(keys))))

    def all_sums(r):
        sums = chip_sums(r, out0, out1)
        return sums[0] + swap_line(sums[1].astype(link)).astype(wide) if lines > 1 else sums[0]

    def onward(move, value):
        return move(value.astype(link)).astype(wide)

    got_up = got_down = 0.0
    for d in range(nearer, 0, -1):
        got_up = onward(to_above, all_sums(d) + got_up)
        if depth - d > nearer:
            got_down = onward(to_below, all_sums(depth - d) + got_down)
    return (all_sums(0) + got_up + got_down).astype(jnp.bfloat16)


def solution(mesh):
    groups, owners = mesh.shape["grp"], mesh.shape["exp"]
    lines = max(1, 4 // groups)
    depth = owners // (lines * CORES)
    in_specs = (
        P(("grp", "exp"), None),
        P(("grp", "exp"), None),
        P(("grp", "exp"), None),
        P("exp", None, None),
        P("exp", None, None),
        P("exp", None, None),
    )
    out_specs = P(("grp", "exp"), None)
    return jax.shard_map(
        functools.partial(body, depth, lines),
        mesh=mesh,
        in_specs=in_specs,
        out_specs=out_specs,
        check_vma=False,
    )
```

```python
import functools

import jax
import jax.numpy as jnp
from jax import lax
from jax.experimental import pallas as pl
from jax.experimental.pallas import tpu as pltpu
from jax.sharding import PartitionSpec as P

CAP = 24
CORES = 2
LANES = 128
LONG = 40_000_000_000
MIB = 1024 * 1024
SMALL_LIMIT = 6 * MIB


def params(limit=SMALL_LIMIT):
    return pltpu.CompilerParams(vmem_limit_bytes=limit)


def selector(code_ref, local):
    row = jnp.concatenate([code_ref[0, local : local + 1, :], code_ref[1, local : local + 1, :] + CAP], axis=1)
    slots = lax.broadcasted_iota(jnp.int32, (2 * CAP, row.shape[1]), 0)
    return row == slots


def picks(code_ref):
    hits = [selector(code_ref, local) for local in range(code_ref.shape[1])]
    return jnp.concatenate([jnp.where(hit, 1.0, 0.0).astype(jnp.bfloat16) for hit in hits], axis=0)


def routes_kernel(ids_ref, weight_ref, tokens_ref, out_ref):
    top, tok = ids_ref.shape
    high = weight_ref[...].astype(jnp.bfloat16).astype(jnp.float32)
    rest = weight_ref[...] - high
    middle = rest.astype(jnp.bfloat16).astype(jnp.float32)
    routes = jnp.concatenate([ids_ref[...].astype(jnp.float32), high, middle, rest - middle], axis=0)
    out_ref[:, :LANES] = jnp.zeros((out_ref.shape[0], LANES), jnp.bfloat16)
    out_ref[: 4 * top, :tok] = routes.astype(jnp.bfloat16)
    out_ref[:, LANES:] = tokens_ref[...]


def with_routes(tokens, expert_ids, route_weight):
    tok, width = tokens.shape
    return pl.pallas_call(
        routes_kernel,
        out_shape=jax.ShapeDtypeStruct((tok, LANES + width), jnp.bfloat16),
        compiler_params=params(58 * MIB),
        cost_estimate=pl.CostEstimate(flops=0, bytes_accessed=0, transcendentals=0),
    )(expert_ids.T, route_weight.T, tokens)


def dispatch_kernel(top, first_ref, x0_ref, x1_ref, rows_ref, code_ref, weight_ref):
    local_experts = rows_ref.shape[0]
    tok = x0_ref.shape[0]
    first = first_ref[0]
    members, wts = [], []
    for x_ref in (x0_ref, x1_ref):
        routes = x_ref[: 4 * top, :tok].astype(jnp.float32)
        ids = routes[:top].astype(jnp.int32)
        wt = routes[top : 2 * top] + (routes[2 * top : 3 * top] + routes[3 * top : 4 * top])
        for local in range(local_experts):
            hit = ids == first + local
            members.append(jnp.sum(jnp.where(hit, 1.0, 0.0), axis=0, keepdims=True))
            wts.append(jnp.sum(jnp.where(hit, wt, 0.0), axis=0, keepdims=True))
    pad = -len(members) % 16
    member = jnp.concatenate(members + [jnp.zeros((pad, tok), jnp.float32)] * (pad > 0), axis=0)
    before = lax.broadcasted_iota(jnp.int32, (tok, tok), 0) < lax.broadcasted_iota(jnp.int32, (tok, tok), 1)
    rank = jnp.dot(
        member.astype(jnp.bfloat16),
        jnp.where(before, 1.0, 0.0).astype(jnp.bfloat16),
        preferred_element_type=jnp.float32,
    )
    code = jnp.where(member > 0.0, rank.astype(jnp.int32), -1024)
    for i in range(2):
        for local in range(local_experts):
            n = i * local_experts + local
            code_ref[i, local : local + 1, :] = code[n : n + 1]
    for local in range(local_experts):
        wt = jnp.concatenate([wts[local], wts[local_experts + local]], axis=1)
        weight = jnp.sum(jnp.where(selector(code_ref, local), wt, 0.0), axis=1, keepdims=True)
        weight_ref[local] = jnp.broadcast_to(weight, weight_ref.shape[1:])
    pick_rows(code_ref, x0_ref[:, LANES:], x1_ref[:, LANES:], rows_ref)


def pick_rows(code_ref, x0, x1, rows_ref):
    x = jnp.concatenate([x0, x1], axis=0)
    rows = jnp.dot(picks(code_ref), x, preferred_element_type=jnp.float32).astype(jnp.bfloat16)
    rows_ref[...] = rows.reshape(rows_ref.shape)


def more_kernel(code_ref, x0_ref, x1_ref, rows_ref):
    pick_rows(code_ref, x0_ref[...], x1_ref[...], rows_ref)


def pick_cost(local_experts, tok, width):
    return pl.CostEstimate(
        flops=8 * local_experts * CAP * tok * width,
        bytes_accessed=4 * width * (tok + local_experts * CAP),
        transcendentals=0,
    )


def dispatch(first, top, local_experts, x0, x1):
    tok, width = x0.shape[0], x0.shape[1] - LANES
    whole = pl.BlockSpec(memory_space=pltpu.VMEM)
    return pl.pallas_call(
        functools.partial(dispatch_kernel, top),
        in_specs=[pl.BlockSpec(memory_space=pltpu.SMEM), whole, whole],
        out_specs=(whole,) * 3,
        out_shape=(
            jax.ShapeDtypeStruct((local_experts, 2 * CAP, width), jnp.bfloat16),
            jax.ShapeDtypeStruct((2, local_experts, tok), jnp.int32),
            jax.ShapeDtypeStruct((local_experts, 2 * CAP, LANES), jnp.float32),
        ),
        compiler_params=params(),
        cost_estimate=pl.CostEstimate(flops=0, bytes_accessed=0, transcendentals=0),
    )(first, x0, x1)


def dispatch_more(code, x0, x1):
    local_experts, width = code.shape[1], x0.shape[1]
    return pl.pallas_call(
        more_kernel,
        out_shape=jax.ShapeDtypeStruct((local_experts, 2 * CAP, width), jnp.bfloat16),
        compiler_params=params(),
        cost_estimate=pl.CostEstimate(flops=0, bytes_accessed=0, transcendentals=0),
    )(code, x0, x1)


def row_blocks(pairs):
    return [range(p, min(p + 8, pairs)) for p in range(0, pairs, 8)]


def columns_of(refs, first, last):
    return [slice(first, last) if r.shape[2] > last - first else slice(None) for r in refs]


def rows_of(refs, local, first, last, block):
    where = columns_of(refs, first, last)
    return jnp.concatenate([refs[p][local, :, where[p]] for p in block], axis=0)


def span(block):
    return slice(block[0] * 2 * CAP, (block[-1] + 1) * 2 * CAP)


class Stream:
    def __init__(self, hbm, buffer, sems, rows, columns):
        self.hbm, self.buffer, self.sems, self.where = hbm, buffer, sems, (rows, columns)

    def copy(self, local):
        return pltpu.make_async_copy(self.hbm.at[(local,) + self.where], self.buffer.at[local], self.sems.at[local])

    def start(self, local):
        self.copy(local).start()

    def get(self, local):
        self.copy(local).wait()
        return self.buffer[local]


def over_experts(count, streams, work):
    for local in range(count):
        for stream in streams:
            stream.start(local)
    pl.loop(0, count)(work)


def stream_scratch(count, *shapes):
    buffers = [pltpu.VMEM((count,) + shape, jnp.bfloat16) for shape in shapes]
    return buffers + [pltpu.SemaphoreType.DMA((count,)) for _ in shapes]


def begin_kernel(pairs, part, token_ref, *refs):
    rows_refs = refs[:pairs]
    gate_hbm, up_hbm, gate_ref, up_ref, gate_buf, up_buf, gate_sem, up_sem = refs[pairs:]
    head, full = slice(0, part), slice(None)
    gate_w = Stream(gate_hbm, gate_buf, gate_sem, head, full)
    up_w = Stream(up_hbm, up_buf, up_sem, head, full)

    def work(local):
        blocks = row_blocks(pairs)
        for stream, out_ref in ((gate_w, gate_ref), (up_w, up_ref)):
            weight = stream.get(local)
            for block in blocks:
                rows = rows_of(rows_refs, local, 0, part, block)
                out_ref[local, span(block)] = jnp.dot(rows, weight, preferred_element_type=jnp.float32)

    over_experts(gate_ref.shape[0], (gate_w, up_w), work)


VMEM_SPEC = pl.BlockSpec(memory_space=pltpu.VMEM)
HBM_SPEC = pl.BlockSpec(memory_space=pltpu.HBM)


def begin(token, rows, part, w_gate, w_up):
    pairs = len(rows)
    local_experts, _, hidden = w_gate.shape
    count = pairs * 2 * CAP
    shape = jax.ShapeDtypeStruct((local_experts, count, hidden), jnp.float32)
    return pl.pallas_call(
        functools.partial(begin_kernel, pairs, part),
        in_specs=[VMEM_SPEC] * (pairs + 1) + [HBM_SPEC] * 2,
        out_specs=(VMEM_SPEC,) * 2,
        out_shape=(shape, shape),
        scratch_shapes=stream_scratch(local_experts, (part, hidden), (part, hidden)),
        compiler_params=params(32 * MIB),
        cost_estimate=pl.CostEstimate(flops=LONG, bytes_accessed=0, transcendentals=0),
    )(token, *rows, w_gate, w_up)


def middle_kernel(pairs, cut, part, *refs):
    rows_refs, weight_refs = refs[:pairs], refs[pairs : 2 * pairs]
    gate_sum, up_sum, gate_hbm, up_hbm, down_hbm, hidden_ref = refs[2 * pairs : 2 * pairs + 6]
    out_refs, scratch = refs[2 * pairs + 6 : 3 * pairs + 6], refs[3 * pairs + 6 :]
    tail, full = slice(cut, gate_hbm.shape[1]), slice(None)
    gate_w = Stream(gate_hbm, scratch[0], scratch[3], tail, full)
    up_w = Stream(up_hbm, scratch[1], scratch[4], tail, full)
    down_w = Stream(down_hbm, scratch[2], scratch[5], full, slice(0, part))

    def work(local):
        gate_now, up_now, down_now = gate_w.get(local), up_w.get(local), None
        for block in row_blocks(pairs):
            rows = rows_of(rows_refs, local, cut, gate_hbm.shape[1], block)
            weight = jnp.concatenate([weight_refs[p][local, :, :1] for p in block], axis=0)
            at = span(block)
            gate = gate_sum[local, at] + jnp.dot(rows, gate_now, preferred_element_type=jnp.float32)
            up = up_sum[local, at] + jnp.dot(rows, up_now, preferred_element_type=jnp.float32)
            hidden = (gate / (1.0 + jnp.exp(-gate)) * up * weight).astype(jnp.bfloat16)
            hidden_ref[local, at] = hidden
            if down_now is None:
                down_now = down_w.get(local)
            write_out(out_refs, local, block, hidden, down_now)

    over_experts(hidden_ref.shape[0], (gate_w, up_w, down_w), work)


def write_out(out_refs, local, block, hidden, weight):
    out = jnp.dot(hidden, weight, preferred_element_type=jnp.float32).astype(jnp.bfloat16)
    for i, p in enumerate(block):
        out_refs[p][local] = out[i * 2 * CAP : (i + 1) * 2 * CAP]


def middle(rows, cut, part, weights, gate_sum, up_sum, w_gate, w_up, w_down):
    pairs = len(rows)
    local_experts, width, hidden = w_gate.shape
    count = pairs * 2 * CAP
    out_shapes = [jax.ShapeDtypeStruct((local_experts, 2 * CAP, part), jnp.bfloat16)] * pairs
    got = pl.pallas_call(
        functools.partial(middle_kernel, pairs, cut, part),
        in_specs=[VMEM_SPEC] * (2 * pairs + 2) + [HBM_SPEC] * 3,
        out_specs=[VMEM_SPEC] * (pairs + 1),
        out_shape=[jax.ShapeDtypeStruct((local_experts, count, hidden), jnp.bfloat16)] + out_shapes,
        scratch_shapes=stream_scratch(local_experts, (width - cut, hidden), (width - cut, hidden), (hidden, part)),
        compiler_params=params(32 * MIB),
        cost_estimate=pl.CostEstimate(flops=0, bytes_accessed=0, transcendentals=0),
    )(*rows, *weights, gate_sum, up_sum, w_gate, w_up, w_down)
    return got[0], got[1:]


def finish_kernel(pairs, part, hidden_ref, down_hbm, *refs):
    out_refs, (buffer, sem) = refs[:pairs], refs[pairs:]
    down_w = Stream(down_hbm, buffer, sem, slice(None), slice(part, 2 * part))

    def work(local):
        weight = down_w.get(local)
        for block in row_blocks(pairs):
            write_out(out_refs, local, block, hidden_ref[local, span(block)], weight)

    over_experts(hidden_ref.shape[0], (down_w,), work)


def finish(hidden, w_down, part, pairs):
    local_experts, count, depth = hidden.shape
    return pl.pallas_call(
        functools.partial(finish_kernel, pairs, part),
        in_specs=[VMEM_SPEC, HBM_SPEC],
        out_specs=[VMEM_SPEC] * pairs,
        out_shape=[jax.ShapeDtypeStruct((local_experts, 2 * CAP, part), jnp.bfloat16)] * pairs,
        scratch_shapes=stream_scratch(local_experts, (depth, part)),
        compiler_params=params(46 * MIB),
        cost_estimate=pl.CostEstimate(flops=0, bytes_accessed=0, transcendentals=0),
    )(hidden, w_down)


def combine_kernel(code_ref, *refs):
    out_refs, (y0_ref, y1_ref) = refs[:-2], refs[-2:]
    pick = picks(code_ref)
    for i, out_ref in enumerate(out_refs):
        local_experts, slots, width = out_ref.shape
        out = out_ref[...].reshape(local_experts * slots, width)
        y = lax.dot_general(pick, out, (((0,), (0,)), ((), ())), preferred_element_type=jnp.float32)
        tok = y0_ref.shape[0]
        y0_ref[:, i * width : (i + 1) * width] = y[:tok]
        y1_ref[:, i * width : (i + 1) * width] = y[tok:].astype(jnp.bfloat16)


def combine(code, *results):
    local_experts, slots, _ = results[0].shape
    width = sum(r.shape[2] for r in results)
    tok = code.shape[2]
    return pl.pallas_call(
        combine_kernel,
        out_shape=(
            jax.ShapeDtypeStruct((tok, width), jnp.float32),
            jax.ShapeDtypeStruct((tok, width), jnp.bfloat16),
        ),
        compiler_params=params(),
        cost_estimate=pl.CostEstimate(flops=0, bytes_accessed=0, transcendentals=0),
    )(code, *results)


def after(value, *others):
    return lax.optimization_barrier((value, *others))[0]


def fence_kernel(in_ref, out_ref):
    out_ref[...] = in_ref[...] + 1.0


def tie(*values):
    return lax.optimization_barrier(values)


def fence(token, *later):
    token = pl.pallas_call(
        fence_kernel,
        out_shape=jax.ShapeDtypeStruct(token.shape, token.dtype),
        compiler_params=params(),
        cost_estimate=pl.CostEstimate(flops=LONG, bytes_accessed=0, transcendentals=0),
    )(token)
    return tie(token, *later)


def last_kernel(token_ref, a_ref, *refs):
    refs, out_ref = refs[:-1], refs[-1]
    total = a_ref[...]
    for ref in refs:
        total += ref[...].astype(jnp.float32)
    out_ref[...] = total.astype(out_ref.dtype)


def last_sum(token, *terms):
    return pl.pallas_call(
        last_kernel,
        in_specs=[VMEM_SPEC] * (1 + len(terms)),
        out_shape=jax.ShapeDtypeStruct(terms[0].shape, jnp.bfloat16),
        compiler_params=params(),
        cost_estimate=pl.CostEstimate(flops=0, bytes_accessed=0, transcendentals=0),
    )(token, *terms)


def body(depth, lines, tokens, expert_ids, route_weight, w_gate, w_up, w_down):
    width = tokens.shape[1]
    top = expert_ids.shape[1]
    local_experts = w_gate.shape[0]
    index = lax.axis_index("exp")
    part = width // 2
    cut = width * 3 // 8

    def place(pz, py, pc):
        return (pz % depth * lines + py) * CORES + pc

    everyone = [(a, b, c) for a in range(depth) for b in range(lines) for c in range(CORES)]

    def send(value, move):
        return lax.ppermute(value, "exp", [(place(*who), place(*move(*who))) for who in everyone])

    def swap_core(value):
        return send(value, lambda a, b, c: (a, b, 1 - c))

    def swap_line(value):
        return send(value, lambda a, b, c: (a, 1 - b, c))

    def to_above(value):
        return send(value, lambda a, b, c: (a + 1, b, c))

    def to_below(value):
        return send(value, lambda a, b, c: (a - 1, b, c))

    nearer = depth // 2
    line = [with_routes(tokens, expert_ids, route_weight)] + [None] * (depth - 1)
    turns = []
    for d in range(1, nearer + 1):
        turns.append((d, d - 1, to_below))
        if depth - d > nearer:
            turns.append((depth - d, (depth - d + 1) % depth, to_above))
    first = (index * local_experts).astype(jnp.int32).reshape(1)
    rows, codes, weights, late = {}, {}, {}, {}

    def take(key, piece, other):
        halves = piece if isinstance(piece, list) else [piece]
        rows[key], codes[key], weights[key] = dispatch(first, top, local_experts, halves[0], other)
        if len(halves) > 1:
            late[key] = halves[1]

    if lines > 1 and depth == 4:
        line[1], far = to_below(line[0]), {0: swap_line(line[0])}
        others = {(0, 0): swap_core(line[0])}
        token, line[0] = fence(jnp.zeros((8, LANES), jnp.float32), line[0])
        line[3] = to_above(line[0])
        token, line[1], others[0, 0] = fence(token, line[1], others[0, 0])
        far[1], others[1, 0] = swap_line(line[1]), swap_core(line[1])
        token, line[1] = fence(token, line[1])
        line[2] = to_below(line[1])
        take((0, 0), line[0], others[0, 0])
        token, line[1], rows[0, 0] = tie(token, line[1], rows[0, 0])
        token, line[3], far[0], others[1, 0] = fence(token, line[3], far[0], others[1, 0])
        far[3] = swap_line(line[3])
        others[3, 0], others[0, 1] = swap_core(line[3]), swap_core(far[0])
        take((1, 0), line[1], others[1, 0])
        token, line[3], far[0], rows[1, 0] = tie(token, line[3], far[0], rows[1, 0])
        others[1, 1] = swap_core(far[1])
        token, line[2], others[3, 0], others[0, 1], others[1, 1] = fence(
            token, line[2], others[3, 0], others[0, 1], others[1, 1]
        )
        head, tail = swap_line(line[2][:, : LANES + cut]), swap_line(line[2][:, LANES + cut :])
        others[2, 0] = swap_core(line[2])
        for key, piece in (((3, 0), line[3]), ((0, 1), far[0]), ((1, 1), far[1])):
            take(key, piece, others[key])
        token, rows[3, 0], rows[0, 1], rows[1, 1] = tie(token, rows[3, 0], rows[0, 1], rows[1, 1])
        token, far[3], head = fence(token, far[3], head)
        others[3, 1], others[2, 1] = swap_core(far[3]), swap_core(head)
        take((2, 0), line[2], others[2, 0])
        take((3, 1), far[3], others[3, 1])
        take((2, 1), [head, tail], others[2, 1])
    else:
        token = jnp.zeros((8, LANES), jnp.float32)
        for r, source, move in turns:
            line[r] = move(line[source])
        for r in range(depth):
            take((r, 0), line[r], swap_core(line[r]))
            if lines > 1:
                piece = swap_line(line[r])
                take((r, 1), piece, swap_core(piece))
    keys = sorted(rows)

    gate_sum, up_sum = begin(token, [rows[k] for k in keys], cut, w_gate, w_up)
    for key, half in late.items():
        half, gate_sum, up_sum = lax.optimization_barrier((half, gate_sum, up_sum))
        rows[key] = dispatch_more(codes[key], half, swap_core(half))
    hidden, out0 = middle(
        [rows[k] for k in keys], cut, part, [weights[k] for k in keys], gate_sum, up_sum, w_gate, w_up, w_down
    )
    out0 = dict(zip(keys, out0))

    wide = jnp.float32
    link = jnp.bfloat16 if depth <= 4 else wide

    def chip_sums(r, *parts):
        sums = []
        for b in reversed(range(lines)):
            y0, y1 = combine(codes[r, b], *[part[r, b] for part in parts])
            sums.append(y0 + swap_core(y1).astype(wide))
        return sums[::-1]

    def lined(sums):
        return sums[0] + swap_line(sums[1].astype(link)).astype(wide) if lines > 1 else sums[0]

    if lines > 1 and depth == 4:
        early = chip_sums(2, out0)
        token, first_half, hidden = tie(token, early[1].astype(link), hidden)
        cross2 = swap_line(first_half)
        token, hidden = fence(token, hidden)
        out1 = dict(zip(keys, finish(hidden, w_down, part, len(keys))))
        token, out1[2, 1] = tie(token, out1[2, 1])
        rest = [(1, 0), (1, 1), (0, 0), (0, 1)]
        half, third = chip_sums(2, out1), chip_sums(3, out0, out1)
        aside, cross3, *tied = tie(half[1].astype(link), third[1].astype(link), *[codes[k] for k in rest])
        codes.update(zip(rest, tied))
        aside, cross3, ahead = to_above(aside), swap_line(cross3), to_above(half[0].astype(link))
        token, cross2 = fence(token, cross2)
        behind = to_above((early[0] + cross2).astype(link))
        nearest, own = chip_sums(1, out0, out1), chip_sums(0, out0, out1)
        token, aside = fence(token, aside)
        cross1 = jnp.concatenate([nearest[1][:, :part], nearest[1][:, part:] + aside], axis=1).astype(link)
        cross1 = swap_line(cross1)
        token, last, cross3 = fence(token, own[1].astype(link), cross3)
        below = to_below((third[0] + cross3).astype(link))
        cross0 = swap_line(last)
        token, cross1, behind, ahead = fence(token, cross1, behind, ahead)
        above = to_above((nearest[0] + cross1 + jnp.concatenate([behind, ahead], axis=1)).astype(link))
        return last_sum(token, own[0], cross0, above, below)

    out1 = dict(zip(keys, finish(hidden, w_down, part, len(keys))))

    def all_sums(r):
        sums = chip_sums(r, out0, out1)
        return sums[0] + swap_line(sums[1].astype(link)).astype(wide) if lines > 1 else sums[0]

    def onward(move, value):
        return move(value.astype(link)).astype(wide)

    got_up = got_down = 0.0
    for d in range(nearer, 0, -1):
        got_up = onward(to_above, all_sums(d) + got_up)
        if depth - d > nearer:
            got_down = onward(to_below, all_sums(depth - d) + got_down)
    return (all_sums(0) + got_up + got_down).astype(jnp.bfloat16)


def solution(mesh):
    groups, owners = mesh.shape["grp"], mesh.shape["exp"]
    lines = max(1, 4 // groups)
    depth = owners // (lines * CORES)
    in_specs = (
        P(("grp", "exp"), None),
        P(("grp", "exp"), None),
        P(("grp", "exp"), None),
        P("exp", None, None),
        P("exp", None, None),
        P("exp", None, None),
    )
    out_specs = P(("grp", "exp"), None)
    return jax.shard_map(
        functools.partial(body, depth, lines),
        mesh=mesh,
        in_specs=in_specs,
        out_specs=out_specs,
        check_vma=False,
    )
```

```python
import functools

import jax
import jax.numpy as jnp
from jax import lax
from jax.experimental import pallas as pl
from jax.experimental.pallas import tpu as pltpu
from jax.sharding import PartitionSpec as P

CAP = 24
CORES = 2
LANES = 128
LONG = 40_000_000_000
MIB = 1024 * 1024
SMALL_LIMIT = 6 * MIB


def params(limit=SMALL_LIMIT):
    return pltpu.CompilerParams(vmem_limit_bytes=limit)


def selector(code_ref, local):
    row = jnp.concatenate([code_ref[0, local : local + 1, :], code_ref[1, local : local + 1, :] + CAP], axis=1)
    slots = lax.broadcasted_iota(jnp.int32, (2 * CAP, row.shape[1]), 0)
    return row == slots


def picks(code_ref):
    hits = [selector(code_ref, local) for local in range(code_ref.shape[1])]
    return jnp.concatenate([jnp.where(hit, 1.0, 0.0).astype(jnp.bfloat16) for hit in hits], axis=0)


def routes_kernel(ids_ref, weight_ref, tokens_ref, out_ref):
    top, tok = ids_ref.shape
    high = weight_ref[...].astype(jnp.bfloat16).astype(jnp.float32)
    rest = weight_ref[...] - high
    middle = rest.astype(jnp.bfloat16).astype(jnp.float32)
    routes = jnp.concatenate([ids_ref[...].astype(jnp.float32), high, middle, rest - middle], axis=0)
    out_ref[:, :LANES] = jnp.zeros((out_ref.shape[0], LANES), jnp.bfloat16)
    out_ref[: 4 * top, :tok] = routes.astype(jnp.bfloat16)
    out_ref[:, LANES:] = tokens_ref[...]


def with_routes(tokens, expert_ids, route_weight):
    tok, width = tokens.shape
    return pl.pallas_call(
        routes_kernel,
        out_shape=jax.ShapeDtypeStruct((tok, LANES + width), jnp.bfloat16),
        compiler_params=params(58 * MIB),
        cost_estimate=pl.CostEstimate(flops=0, bytes_accessed=0, transcendentals=0),
    )(expert_ids.T, route_weight.T, tokens)


def dispatch_kernel(top, first_ref, x0_ref, x1_ref, rows_ref, code_ref, weight_ref):
    local_experts = rows_ref.shape[0]
    tok = x0_ref.shape[0]
    first = first_ref[0]
    members, wts = [], []
    for x_ref in (x0_ref, x1_ref):
        routes = x_ref[: 4 * top, :tok].astype(jnp.float32)
        ids = routes[:top].astype(jnp.int32)
        wt = routes[top : 2 * top] + (routes[2 * top : 3 * top] + routes[3 * top : 4 * top])
        for local in range(local_experts):
            hit = ids == first + local
            members.append(jnp.sum(jnp.where(hit, 1.0, 0.0), axis=0, keepdims=True))
            wts.append(jnp.sum(jnp.where(hit, wt, 0.0), axis=0, keepdims=True))
    pad = -len(members) % 16
    member = jnp.concatenate(members + [jnp.zeros((pad, tok), jnp.float32)] * (pad > 0), axis=0)
    before = lax.broadcasted_iota(jnp.int32, (tok, tok), 0) < lax.broadcasted_iota(jnp.int32, (tok, tok), 1)
    rank = jnp.dot(
        member.astype(jnp.bfloat16),
        jnp.where(before, 1.0, 0.0).astype(jnp.bfloat16),
        preferred_element_type=jnp.float32,
    )
    code = jnp.where(member > 0.0, rank.astype(jnp.int32), -1024)
    for i in range(2):
        for local in range(local_experts):
            n = i * local_experts + local
            code_ref[i, local : local + 1, :] = code[n : n + 1]
    for local in range(local_experts):
        wt = jnp.concatenate([wts[local], wts[local_experts + local]], axis=1)
        weight = jnp.sum(jnp.where(selector(code_ref, local), wt, 0.0), axis=1, keepdims=True)
        weight_ref[local] = jnp.broadcast_to(weight, weight_ref.shape[1:])
    pick_rows(code_ref, x0_ref[:, LANES:], x1_ref[:, LANES:], rows_ref)


def pick_rows(code_ref, x0, x1, rows_ref):
    x = jnp.concatenate([x0, x1], axis=0)
    rows = jnp.dot(picks(code_ref), x, preferred_element_type=jnp.float32).astype(jnp.bfloat16)
    rows_ref[...] = rows.reshape(rows_ref.shape)


def more_kernel(code_ref, x0_ref, x1_ref, rows_ref):
    pick_rows(code_ref, x0_ref[...], x1_ref[...], rows_ref)


def pick_cost(local_experts, tok, width):
    return pl.CostEstimate(
        flops=8 * local_experts * CAP * tok * width,
        bytes_accessed=4 * width * (tok + local_experts * CAP),
        transcendentals=0,
    )


def dispatch(first, top, local_experts, x0, x1):
    tok, width = x0.shape[0], x0.shape[1] - LANES
    whole = pl.BlockSpec(memory_space=pltpu.VMEM)
    return pl.pallas_call(
        functools.partial(dispatch_kernel, top),
        in_specs=[pl.BlockSpec(memory_space=pltpu.SMEM), whole, whole],
        out_specs=(whole,) * 3,
        out_shape=(
            jax.ShapeDtypeStruct((local_experts, 2 * CAP, width), jnp.bfloat16),
            jax.ShapeDtypeStruct((2, local_experts, tok), jnp.int32),
            jax.ShapeDtypeStruct((local_experts, 2 * CAP, LANES), jnp.float32),
        ),
        compiler_params=params(),
        cost_estimate=pl.CostEstimate(flops=0, bytes_accessed=0, transcendentals=0),
    )(first, x0, x1)


def dispatch_more(code, x0, x1):
    local_experts, width = code.shape[1], x0.shape[1]
    return pl.pallas_call(
        more_kernel,
        out_shape=jax.ShapeDtypeStruct((local_experts, 2 * CAP, width), jnp.bfloat16),
        compiler_params=params(),
        cost_estimate=pl.CostEstimate(flops=0, bytes_accessed=0, transcendentals=0),
    )(code, x0, x1)


def row_blocks(pairs):
    return [range(p, min(p + 8, pairs)) for p in range(0, pairs, 8)]


def columns_of(refs, first, last):
    return [slice(first, last) if r.shape[2] > last - first else slice(None) for r in refs]


def rows_of(refs, local, first, last, block):
    where = columns_of(refs, first, last)
    return jnp.concatenate([refs[p][local, :, where[p]] for p in block], axis=0)


def span(block):
    return slice(block[0] * 2 * CAP, (block[-1] + 1) * 2 * CAP)


class Stream:
    def __init__(self, hbm, buffer, sems, rows, columns, given=None):
        self.given = given
        self.hbm, self.buffer, self.sems, self.where = hbm, buffer, sems, (rows, columns)

    def copy(self, local):
        return pltpu.make_async_copy(self.hbm.at[(local,) + self.where], self.buffer.at[local], self.sems.at[local])

    def start(self, local):
        self.copy(local).start()

    def get(self, local):
        if self.given and isinstance(local, int):
            return self.given[0][...]
        self.copy(local).wait()
        return self.buffer[local]


def over_experts(count, streams, work, others=()):
    for local in range(count):
        for stream in streams:
            if local or not stream.given:
                stream.start(local)
    for copy in others:
        copy.start()
    if any(stream.given for stream in streams):
        work(0)
        if count > 1:
            pl.loop(1, count)(work)
    else:
        pl.loop(0, count)(work)


def stream_scratch(count, *shapes):
    buffers = [pltpu.VMEM((count,) + shape, jnp.bfloat16) for shape in shapes]
    return buffers + [pltpu.SemaphoreType.DMA((count,)) for _ in shapes]


def begin_kernel(pairs, part, token_ref, *refs):
    rows_refs = refs[:pairs]
    gate_hbm, up_hbm, gate_ref, up_ref, *ahead = refs[pairs : pairs + 6]
    gate_buf, up_buf, gate_sem, up_sem, ahead_sem = refs[pairs + 6 :]
    head, full = slice(0, part), slice(None)
    gate_w = Stream(gate_hbm, gate_buf, gate_sem, head, full)
    up_w = Stream(up_hbm, up_buf, up_sem, head, full)

    def work(local):
        blocks = row_blocks(pairs)
        for stream, out_ref in ((gate_w, gate_ref), (up_w, up_ref)):
            weight = stream.get(local)
            for block in blocks:
                rows = rows_of(rows_refs, local, 0, part, block)
                out_ref[local, span(block)] = jnp.dot(rows, weight, preferred_element_type=jnp.float32)

    copies = [
        pltpu.make_async_copy(hbm.at[0, slice(part, hbm.shape[1]), :], out, ahead_sem.at[i])
        for i, (hbm, out) in enumerate(zip((gate_hbm, up_hbm), ahead))
    ]
    over_experts(gate_ref.shape[0], (gate_w, up_w), work, copies)
    for copy in copies:
        copy.wait()


VMEM_SPEC = pl.BlockSpec(memory_space=pltpu.VMEM)
HBM_SPEC = pl.BlockSpec(memory_space=pltpu.HBM)


def begin(token, rows, part, w_gate, w_up):
    pairs = len(rows)
    local_experts, width, hidden = w_gate.shape
    count = pairs * 2 * CAP
    shape = jax.ShapeDtypeStruct((local_experts, count, hidden), jnp.float32)
    ahead = jax.ShapeDtypeStruct((width - part, hidden), jnp.bfloat16)
    return pl.pallas_call(
        functools.partial(begin_kernel, pairs, part),
        in_specs=[VMEM_SPEC] * (pairs + 1) + [HBM_SPEC] * 2,
        out_specs=(VMEM_SPEC,) * 4,
        out_shape=(shape, shape, ahead, ahead),
        scratch_shapes=stream_scratch(local_experts, (part, hidden), (part, hidden)) + [pltpu.SemaphoreType.DMA((2,))],
        compiler_params=params(28 * MIB),
        cost_estimate=pl.CostEstimate(flops=LONG, bytes_accessed=0, transcendentals=0),
    )(token, *rows, w_gate, w_up)


def middle_kernel(pairs, cut, part, *refs):
    rows_refs, weight_refs = refs[:pairs], refs[pairs : 2 * pairs]
    gate_sum, up_sum, gate_first, up_first, gate_hbm, up_hbm, down_hbm, hidden_ref = refs[2 * pairs : 2 * pairs + 8]
    out_refs, scratch = refs[2 * pairs + 8 : 3 * pairs + 8], refs[3 * pairs + 8 :]
    tail, full = slice(cut, gate_hbm.shape[1]), slice(None)
    gate_w = Stream(gate_hbm, scratch[0], scratch[3], tail, full, [gate_first])
    up_w = Stream(up_hbm, scratch[1], scratch[4], tail, full, [up_first])
    down_w = Stream(down_hbm, scratch[2], scratch[5], full, slice(0, part))

    def work(local):
        gate_now, up_now, down_now = gate_w.get(local), up_w.get(local), None
        for block in row_blocks(pairs):
            rows = rows_of(rows_refs, local, cut, gate_hbm.shape[1], block)
            weight = jnp.concatenate([weight_refs[p][local, :, :1] for p in block], axis=0)
            at = span(block)
            gate = gate_sum[local, at] + jnp.dot(rows, gate_now, preferred_element_type=jnp.float32)
            up = up_sum[local, at] + jnp.dot(rows, up_now, preferred_element_type=jnp.float32)
            hidden = (gate / (1.0 + jnp.exp(-gate)) * up * weight).astype(jnp.bfloat16)
            hidden_ref[local, at] = hidden
            if down_now is None:
                down_now = down_w.get(local)
            write_out(out_refs, local, block, hidden, down_now)

    over_experts(hidden_ref.shape[0], (gate_w, up_w, down_w), work)


def write_out(out_refs, local, block, hidden, weight):
    out = jnp.dot(hidden, weight, preferred_element_type=jnp.float32).astype(jnp.bfloat16)
    for i, p in enumerate(block):
        out_refs[p][local] = out[i * 2 * CAP : (i + 1) * 2 * CAP]


def middle(rows, cut, part, weights, sums, w_gate, w_up, w_down):
    pairs = len(rows)
    local_experts, width, hidden = w_gate.shape
    count = pairs * 2 * CAP
    out_shapes = [jax.ShapeDtypeStruct((local_experts, 2 * CAP, part), jnp.bfloat16)] * pairs
    got = pl.pallas_call(
        functools.partial(middle_kernel, pairs, cut, part),
        in_specs=[VMEM_SPEC] * (2 * pairs + 4) + [HBM_SPEC] * 3,
        out_specs=[VMEM_SPEC] * (pairs + 1),
        out_shape=[jax.ShapeDtypeStruct((local_experts, count, hidden), jnp.bfloat16)] + out_shapes,
        scratch_shapes=stream_scratch(local_experts, (width - cut, hidden), (width - cut, hidden), (hidden, part)),
        compiler_params=params(28 * MIB),
        cost_estimate=pl.CostEstimate(flops=0, bytes_accessed=0, transcendentals=0),
    )(*rows, *weights, *sums, w_gate, w_up, w_down)
    return got[0], got[1:]


def finish_kernel(pairs, part, hidden_ref, down_hbm, *refs):
    out_refs, (buffer, sem) = refs[:pairs], refs[pairs:]
    down_w = Stream(down_hbm, buffer, sem, slice(None), slice(part, 2 * part))

    def work(local):
        weight = down_w.get(local)
        for block in row_blocks(pairs):
            write_out(out_refs, local, block, hidden_ref[local, span(block)], weight)

    over_experts(hidden_ref.shape[0], (down_w,), work)


def finish(hidden, w_down, part, pairs):
    local_experts, count, depth = hidden.shape
    return pl.pallas_call(
        functools.partial(finish_kernel, pairs, part),
        in_specs=[VMEM_SPEC, HBM_SPEC],
        out_specs=[VMEM_SPEC] * pairs,
        out_shape=[jax.ShapeDtypeStruct((local_experts, 2 * CAP, part), jnp.bfloat16)] * pairs,
        scratch_shapes=stream_scratch(local_experts, (depth, part)),
        compiler_params=params(46 * MIB),
        cost_estimate=pl.CostEstimate(flops=0, bytes_accessed=0, transcendentals=0),
    )(hidden, w_down)


def combine_kernel(code_ref, *refs):
    out_refs, (y0_ref, y1_ref) = refs[:-2], refs[-2:]
    pick = picks(code_ref)
    for i, out_ref in enumerate(out_refs):
        local_experts, slots, width = out_ref.shape
        out = out_ref[...].reshape(local_experts * slots, width)
        y = lax.dot_general(pick, out, (((0,), (0,)), ((), ())), preferred_element_type=jnp.float32)
        tok = y0_ref.shape[0]
        y0_ref[:, i * width : (i + 1) * width] = y[:tok]
        y1_ref[:, i * width : (i + 1) * width] = y[tok:].astype(jnp.bfloat16)


def combine(code, *results):
    local_experts, slots, _ = results[0].shape
    width = sum(r.shape[2] for r in results)
    tok = code.shape[2]
    return pl.pallas_call(
        combine_kernel,
        out_shape=(
            jax.ShapeDtypeStruct((tok, width), jnp.float32),
            jax.ShapeDtypeStruct((tok, width), jnp.bfloat16),
        ),
        compiler_params=params(),
        cost_estimate=pl.CostEstimate(flops=0, bytes_accessed=0, transcendentals=0),
    )(code, *results)


def after(value, *others):
    return lax.optimization_barrier((value, *others))[0]


def fence_kernel(in_ref, out_ref):
    out_ref[...] = in_ref[...] + 1.0


def tie(*values):
    return lax.optimization_barrier(values)


def fence(token, *later):
    token = pl.pallas_call(
        fence_kernel,
        out_shape=jax.ShapeDtypeStruct(token.shape, token.dtype),
        compiler_params=params(),
        cost_estimate=pl.CostEstimate(flops=LONG, bytes_accessed=0, transcendentals=0),
    )(token)
    return tie(token, *later)


def last_kernel(token_ref, a_ref, *refs):
    refs, out_ref = refs[:-1], refs[-1]
    total = a_ref[...]
    for ref in refs:
        total += ref[...].astype(jnp.float32)
    out_ref[...] = total.astype(out_ref.dtype)


def last_sum(token, *terms):
    return pl.pallas_call(
        last_kernel,
        in_specs=[VMEM_SPEC] * (1 + len(terms)),
        out_shape=jax.ShapeDtypeStruct(terms[0].shape, jnp.bfloat16),
        compiler_params=params(),
        cost_estimate=pl.CostEstimate(flops=0, bytes_accessed=0, transcendentals=0),
    )(token, *terms)


def body(depth, lines, tokens, expert_ids, route_weight, w_gate, w_up, w_down):
    width = tokens.shape[1]
    top = expert_ids.shape[1]
    local_experts = w_gate.shape[0]
    index = lax.axis_index("exp")
    part = width // 2
    cut = width * 3 // 8

    def place(pz, py, pc):
        return (pz % depth * lines + py) * CORES + pc

    everyone = [(a, b, c) for a in range(depth) for b in range(lines) for c in range(CORES)]

    def send(value, move):
        return lax.ppermute(value, "exp", [(place(*who), place(*move(*who))) for who in everyone])

    def swap_core(value):
        return send(value, lambda a, b, c: (a, b, 1 - c))

    def swap_line(value):
        return send(value, lambda a, b, c: (a, 1 - b, c))

    def to_above(value):
        return send(value, lambda a, b, c: (a + 1, b, c))

    def to_below(value):
        return send(value, lambda a, b, c: (a - 1, b, c))

    nearer = depth // 2
    line = [with_routes(tokens, expert_ids, route_weight)] + [None] * (depth - 1)
    turns = []
    for d in range(1, nearer + 1):
        turns.append((d, d - 1, to_below))
        if depth - d > nearer:
            turns.append((depth - d, (depth - d + 1) % depth, to_above))
    first = (index * local_experts).astype(jnp.int32).reshape(1)
    rows, codes, weights, late = {}, {}, {}, {}

    def take(key, piece, other):
        halves = piece if isinstance(piece, list) else [piece]
        rows[key], codes[key], weights[key] = dispatch(first, top, local_experts, halves[0], other)
        if len(halves) > 1:
            late[key] = halves[1]

    if lines > 1 and depth == 4:
        line[1], others = to_below(line[0]), {(0, 0): swap_core(line[0])}
        token, line[0] = fence(jnp.zeros((8, LANES), jnp.float32), line[0])
        far, line[3] = {0: swap_line(line[0])}, to_above(line[0])
        token, line[1], others[0, 0] = tie(token, line[1], others[0, 0])
        far[1], others[1, 0] = swap_line(line[1]), swap_core(line[1])
        token, line[1] = fence(token, line[1])
        line[2] = to_below(line[1])
        take((0, 0), line[0], others[0, 0])
        token, line[1], rows[0, 0] = tie(token, line[1], rows[0, 0])
        token, line[3], far[0], others[1, 0] = fence(token, line[3], far[0], others[1, 0])
        far[3] = swap_line(line[3])
        others[3, 0], others[0, 1] = swap_core(line[3]), swap_core(far[0])
        take((1, 0), line[1], others[1, 0])
        token, line[3], far[0], rows[1, 0] = tie(token, line[3], far[0], rows[1, 0])
        others[1, 1] = swap_core(far[1])
        token, line[2], others[3, 0], others[0, 1], others[1, 1] = fence(
            token, line[2], others[3, 0], others[0, 1], others[1, 1]
        )
        head, tail = swap_line(line[2][:, : LANES + cut]), swap_line(line[2][:, LANES + cut :])
        others[2, 0] = swap_core(line[2])
        for key, piece in (((3, 0), line[3]), ((0, 1), far[0]), ((1, 1), far[1])):
            take(key, piece, others[key])
        token, rows[3, 0], rows[0, 1], rows[1, 1] = tie(token, rows[3, 0], rows[0, 1], rows[1, 1])
        token, far[3], head = fence(token, far[3], head)
        others[3, 1], others[2, 1] = swap_core(far[3]), swap_core(head)
        take((2, 0), line[2], others[2, 0])
        take((3, 1), far[3], others[3, 1])
        take((2, 1), [head, tail], others[2, 1])
    else:
        token = jnp.zeros((8, LANES), jnp.float32)
        for r, source, move in turns:
            line[r] = move(line[source])
        for r in range(depth):
            take((r, 0), line[r], swap_core(line[r]))
            if lines > 1:
                piece = swap_line(line[r])
                take((r, 1), piece, swap_core(piece))
    keys = sorted(rows)

    sums = begin(token, [rows[k] for k in keys], cut, w_gate, w_up)
    for key, half in late.items():
        half, *sums = lax.optimization_barrier((half, *sums))
        rows[key] = dispatch_more(codes[key], half, swap_core(half))
    hidden, out0 = middle(
        [rows[k] for k in keys], cut, part, [weights[k] for k in keys], sums, w_gate, w_up, w_down
    )
    out0 = dict(zip(keys, out0))

    wide = jnp.float32
    link = jnp.bfloat16 if depth <= 4 else wide

    def chip_sums(r, *parts):
        sums = []
        for b in reversed(range(lines)):
            y0, y1 = combine(codes[r, b], *[part[r, b] for part in parts])
            sums.append(y0 + swap_core(y1).astype(wide))
        return sums[::-1]

    def lined(sums):
        return sums[0] + swap_line(sums[1].astype(link)).astype(wide) if lines > 1 else sums[0]

    if lines > 1 and depth == 4:
        early = chip_sums(2, out0)
        token, first_half, hidden = tie(token, early[1].astype(link), hidden)
        cross2 = swap_line(first_half)
        token, hidden = fence(token, hidden)
        out1 = dict(zip(keys, finish(hidden, w_down, part, len(keys))))
        token, out1[2, 1] = tie(token, out1[2, 1])
        rest = [(1, 0), (1, 1), (0, 0), (0, 1)]
        half, third = chip_sums(2, out1), chip_sums(3, out0, out1)
        aside, cross3, *tied = tie(half[1].astype(link), third[1].astype(link), *[codes[k] for k in rest])
        codes.update(zip(rest, tied))
        aside, cross3, ahead = to_above(aside), swap_line(cross3), to_above(half[0].astype(link))
        token, cross2 = fence(token, cross2)
        behind = to_above((early[0] + cross2).astype(link))
        nearest, own = chip_sums(1, out0, out1), chip_sums(0, out0, out1)
        token, aside = fence(token, aside)
        cross1 = jnp.concatenate([nearest[1][:, :part], nearest[1][:, part:] + aside], axis=1).astype(link)
        cross1 = swap_line(cross1)
        token, last, cross3 = fence(token, own[1].astype(link), cross3)
        below = to_below((third[0] + cross3).astype(link))
        cross0 = swap_line(last)
        token, cross1, behind, ahead = fence(token, cross1, behind, ahead)
        above = to_above((nearest[0] + cross1 + jnp.concatenate([behind, ahead], axis=1)).astype(link))
        return last_sum(token, own[0], cross0, above, below)

    out1 = dict(zip(keys, finish(hidden, w_down, part, len(keys))))

    def all_sums(r):
        sums = chip_sums(r, out0, out1)
        return sums[0] + swap_line(sums[1].astype(link)).astype(wide) if lines > 1 else sums[0]

    def onward(move, value):
        return move(value.astype(link)).astype(wide)

    got_up = got_down = 0.0
    for d in range(nearer, 0, -1):
        got_up = onward(to_above, all_sums(d) + got_up)
        if depth - d > nearer:
            got_down = onward(to_below, all_sums(depth - d) + got_down)
    return (all_sums(0) + got_up + got_down).astype(jnp.bfloat16)


def solution(mesh):
    groups, owners = mesh.shape["grp"], mesh.shape["exp"]
    lines = max(1, 4 // groups)
    depth = owners // (lines * CORES)
    in_specs = (
        P(("grp", "exp"), None),
        P(("grp", "exp"), None),
        P(("grp", "exp"), None),
        P("exp", None, None),
        P("exp", None, None),
        P("exp", None, None),
    )
    out_specs = P(("grp", "exp"), None)
    return jax.shard_map(
        functools.partial(body, depth, lines),
        mesh=mesh,
        in_specs=in_specs,
        out_specs=out_specs,
        check_vma=False,
    )
```
